512 devices in a mesh: rows: 8 (over y, x_lo), cols: 64 (over x_hi, z, core).
Axes of the slice: x: 4 (x_hi: 2, x_lo: 2; x = x_hi * 2 + x_lo), y: 4, z: 16, core: 2. Of those that a mesh axis runs over, the one named last changes fastest.
Arguments:
- fine_in: bfloat16 [64, 4096, 256], P('rows', 'cols'), may hold values from -6 to 6
- mid_in: bfloat16 [32, 2048, 256], P('rows', 'cols'), may hold values from -6 to 6
- coarse_in: bfloat16 [16, 1024, 256], P('rows', 'cols'), may hold values from -6 to 6
- lateral_weight: bfloat16 [768, 256], replicated, may hold values from -0.375 to 0.375
- out_weight: bfloat16 [2304, 256], replicated, may hold values from -0.125 to 0.125
- cotangent: bfloat16 [64, 4096, 256], P('rows', 'cols'), may hold values from -6 to 6
Outputs:
- mask_features: bfloat16 [64, 4096, 256], P('rows', 'cols')
- fine_grad: bfloat16 [64, 4096, 256], P('rows', 'cols')
- mid_grad: bfloat16 [32, 2048, 256], P('rows', 'cols')
- coarse_grad: bfloat16 [16, 1024, 256], P('rows', 'cols')
- lateral_grad: float32 [768, 256], P('cols', 'rows')
- conv_grad: float32 [2304, 256], P('cols', 'rows')
The draws below stay inside these ranges and needn't reach their ends.
All inputs are finite; a program needn't handle non-finite values.
Results may differ from the reference program's by a relative error of at most 0.017.
Values may be sent and summed in bfloat16 or wider, within the bound.
A program may use at most 64 MiB of HBM per device.

```python
import jax
import jax.numpy as jnp
from jax import lax

C = 256
H3 = 64
W3 = 4096


def level_of(rng, shape, shards, low, largest):
    def one(dim, shards_of):
        steps = jax.random.uniform(jax.random.fold_in(jax.random.fold_in(rng, 6), dim), (shards_of,), jnp.float32, low / len(shards), largest / len(shards))
        return jnp.repeat(jnp.exp(steps), shape[dim] // shards_of).reshape((-1,) + (1,) * (len(shape) - dim - 1))

    loudness = one(*shards[0])
    for cut in shards[1:]:
        loudness = loudness * one(*cut)
    return loudness


def gaussian(own_key, dims, scale, limit, split=(), held_as=jnp.bfloat16):
    array = jax.random.normal(own_key, dims, jnp.float32) * scale
    if len(split) > 0:
        array = level_of(own_key, dims, split, -0.22, 0.18) * array
    return jnp.clip(array, min=-limit, max=limit).astype(held_as)


def setup_inputs(seed: int = 0) -> dict:
    key_of = jax.random.split(jax.random.key(seed), 7)
    return {
        "fine_in": gaussian(key_of[0], (H3, W3, C), 1.0, 6.0, ((0, 8), (1, 64))),
        "mid_in": gaussian(key_of[1], (H3 // 2, W3 // 2, C), 1.0, 6.0, ((0, 8), (1, 64))),
        "coarse_in": gaussian(key_of[2], (H3 // 4, W3 // 4, C), 1.0, 6.0, ((0, 8), (1, 64))),
        "lateral_weight": gaussian(key_of[3], (3 * C, C), C ** -0.5, 0.375),
        "out_weight": gaussian(key_of[4], (9 * C, C), (9 * C) ** -0.5, 0.125),
        "cotangent": gaussian(key_of[5], (H3, W3, C), 1.0, 6.0, ((0, 8), (1, 64))),
    }


def lateral(feature, weight):
    height, width, chans = feature.shape
    flat = jnp.dot(feature.reshape(height * width, chans), weight, preferred_element_type=jnp.float32)
    return flat.reshape(height, width, weight.shape[1])

def outer(left, right):
    chans = left.shape[-1]
    return lax.dot_general(left.reshape(-1, chans), right.reshape(-1, right.shape[-1]), (((0,), (0,)), ((), ())), preferred_element_type=jnp.float32)

def widen(coarse, axis):
    count = coarse.shape[axis] - 2
    lower = lax.slice_in_dim(coarse, 0, count, axis=axis)
    middle = lax.slice_in_dim(coarse, 1, count + 1, axis=axis)
    upper = lax.slice_in_dim(coarse, 2, count + 2, axis=axis)
    even = 0.25 * lower + 0.75 * middle
    odd = 0.75 * middle + 0.25 * upper
    joined = jnp.stack([even, odd], axis=axis + 1)
    shape = list(coarse.shape)
    shape[axis] = 2 * count
    return joined.reshape(shape)

def narrow(fine, axis):
    total = fine.shape[axis] - 2
    count = total // 2
    prior_tensor = lax.slice_in_dim(fine, 0, total, axis=axis)
    inner = lax.slice_in_dim(fine, 1, total + 1, axis=axis)
    after = lax.slice_in_dim(fine, 2, total + 2, axis=axis)
    shape = fine.shape[:axis] + (count, 2) + fine.shape[axis + 1:]
    prior_tensor = prior_tensor.reshape(shape)
    inner = inner.reshape(shape)
    after = after.reshape(shape)
    return 0.25 * lax.index_in_dim(prior_tensor, 0, axis + 1, keepdims=False) + 0.75 * lax.index_in_dim(inner, 0, axis + 1, keepdims=False) + 0.75 * lax.index_in_dim(inner, 1, axis + 1, keepdims=False) + 0.25 * lax.index_in_dim(after, 1, axis + 1, keepdims=False)

def edge_pad(receptive_region):
    return jnp.pad(receptive_region, ((1, 1), (1, 1), (0, 0)), mode='edge')

def zero_pad(receptive_region):
    return jnp.pad(receptive_region, ((1, 1), (1, 1), (0, 0)))

def upsample(receptive_region):
    return widen(widen(edge_pad(receptive_region).astype(jnp.float32), 0), 1)

def reduce_resolution(receptive_region):
    return narrow(narrow(edge_pad(receptive_region).astype(jnp.float32), 0), 1)

def gelu_exact(value):
    return jax.nn.gelu(value, approximate=False)

def reference(fine_in, mid_in, coarse_in, lateral_weight, out_weight, cotangent):
    chans = fine_in.shape[-1]
    height, width = (fine_in.shape[0], fine_in.shape[1])
    w_fine = lateral_weight[0:chans]
    w_mid = lateral_weight[chans:2 * chans]
    w_top = lateral_weight[2 * chans:3 * chans]
    top = lateral(coarse_in, w_top).astype(jnp.bfloat16)
    middle = (lateral(mid_in, w_mid) + upsample(top)).astype(jnp.bfloat16)
    fine = (lateral(fine_in, w_fine) + upsample(middle)).astype(jnp.bfloat16)
    padded = zero_pad(fine)
    pre = jnp.zeros((height, width, chans), jnp.float32)
    for tap in range(9):
        row_off, col_off = divmod(tap, 3)
        pre = pre + lateral(padded[row_off:row_off + height, col_off:col_off + width], out_weight[tap * chans:(tap + 1) * chans])
    outputs, pull = jax.vjp(gelu_exact, pre)
    mask_features = outputs.astype(jnp.bfloat16)
    dpre = pull(cotangent.astype(jnp.float32))[0].astype(jnp.bfloat16)
    dpad = zero_pad(dpre)
    fine_level_grad = jnp.zeros((height, width, chans), jnp.float32)
    conv_parts = []
    for tap in range(9):
        row_off, col_off = divmod(tap, 3)
        block = out_weight[tap * chans:(tap + 1) * chans]
        shifted = dpad[2 - row_off:2 - row_off + height, 2 - col_off:2 - col_off + width]
        fine_level_grad = fine_level_grad + lateral(shifted, block.T)
        conv_parts.append(outer(padded[row_off:row_off + height, col_off:col_off + width], dpre))
    fine_level_grad = fine_level_grad.astype(jnp.bfloat16)
    middle_level_grad = reduce_resolution(fine_level_grad).astype(jnp.bfloat16)
    top_level_grad = reduce_resolution(middle_level_grad).astype(jnp.bfloat16)
    fine_grad = lateral(fine_level_grad, w_fine.T).astype(jnp.bfloat16)
    mid_grad = lateral(middle_level_grad, w_mid.T).astype(jnp.bfloat16)
    coarse_grad = lateral(top_level_grad, w_top.T).astype(jnp.bfloat16)
    lateral_grad = jnp.concatenate([outer(fine_in, fine_level_grad), outer(mid_in, middle_level_grad), outer(coarse_in, top_level_grad)], 0)
    conv_grad = jnp.concatenate(conv_parts, 0)
    return (mask_features, fine_grad, mid_grad, coarse_grad, lateral_grad, conv_grad)
```

```python
import functools
from types import SimpleNamespace

import jax
import jax.numpy as jnp
import ml_dtypes
import numpy as np
from jax import lax
from jax.experimental import pallas as pl
from jax.experimental.pallas import tpu as pltpu
from jax.sharding import PartitionSpec as P

BF = jnp.bfloat16
F32 = jnp.float32
MESH = pl.DeviceIdType.MESH
C = 256
NR, NC = 8, 64
LANE = 128


def place(h, w, i, j):
    if j < 0:
        return w * (h + 2) + i + 1
    if j >= w:
        return w * (h + 2) + 16 + i + 1
    return (i + 1) * w + j


def size(h, w):
    return w * (h + 2) + 32


def cells(h, w):
    return [(i, j) for i in range(-1, h + 1) for j in range(-1, w + 1)]


def clamp(i, n, kind):
    if kind == 1:
        i = max(i, 0)
    if kind == 2:
        i = min(i, n - 1)
    return i


def up_taps(i):
    k = i // 2
    if i % 2 == 0:
        return [(k - 1, 0.25), (k, 0.75)]
    return [(k, 0.75), (k + 1, 0.25)]


def up_matrix(h, w, pad):
    mat = np.zeros((9, size(2 * h, 2 * w), pad), np.float32)
    for v in range(9):
        for i, j in cells(2 * h, 2 * w):
            for ri, rw in up_taps(i):
                for ci, cw in up_taps(j):
                    ri2, ci2 = clamp(ri, h, v // 3), clamp(ci, w, v % 3)
                    mat[v, place(2 * h, 2 * w, i, j), place(h, w, ri2, ci2)] += rw * cw
    return mat.astype(ml_dtypes.bfloat16)


def down_matrix(h, w, rows, pad):
    mat = np.zeros((9, rows, pad), np.float32)
    weights = (0.25, 0.75, 0.75, 0.25)
    for v in range(9):
        for i in range(h):
            for j in range(w):
                for a in range(4):
                    for b in range(4):
                        ri = clamp(2 * i - 1 + a, 2 * h, v // 3)
                        ci = clamp(2 * j - 1 + b, 2 * w, v % 3)
                        mat[v, i * w + j, place(2 * h, 2 * w, ri, ci)] += weights[a] * weights[b]
    return mat.astype(ml_dtypes.bfloat16)


def pack_matrix(h, w, first, cols):
    mat = np.zeros((32, cols), np.float32)
    for i in range(h):
        mat[first + i, i * w] = 1
        mat[16 + first + i, i * w + w - 1] = 1
    return mat.astype(ml_dtypes.bfloat16)


def side_matrix(levels):
    mat = np.zeros((32 * len(levels), LANE), np.float32)
    for n, (h, first) in enumerate(levels):
        for side in range(2):
            row, src = 32 * n + 16 * side, 48 * side
            mat[row, src + 16 + first + h - 1] = 1
            for i in range(h):
                mat[row + 1 + i, src + first + i] = 1
            mat[row + 1 + h, src + 32 + first] = 1
    return mat.astype(ml_dtypes.bfloat16)


def constants():
    packs = [
        pack_matrix(8, 64, 0, 512),
        pack_matrix(4, 32, 8, 128),
        pack_matrix(2, 16, 12, 32),
        pack_matrix(4, 32, 0, 128),
    ]
    return dict(
        u1=up_matrix(2, 16, 128),
        u2=up_matrix(4, 32, 256),
        d1=down_matrix(4, 32, 128, 768),
        d2=down_matrix(2, 16, 128, 256),
        pf=packs[0],
        pm=packs[1],
        pc=np.concatenate([packs[2], np.zeros((32, 96), ml_dtypes.bfloat16)], 1),
        pm0=packs[3],
        s1=side_matrix([(8, 0), (4, 8), (2, 12)]),
        sf=side_matrix([(8, 0)]),
        sm=side_matrix([(4, 0)]),
    )


CP, CQ, LP, LQ = 640, 512, 128, 256


def dot(a, b):
    return jnp.dot(a, b, preferred_element_type=F32)


def dot_t(a, b):
    return lax.dot_general(a, b, (((1,), (1,)), ((), ())), preferred_element_type=F32)


def kernel(consts, *refs):
    fin, mid, coa, wl, wo_hbm, cot = refs[:6]
    k = SimpleNamespace(**dict(zip(consts, refs[6 : 6 + len(consts)])))
    o_mask, o_fine, o_mid, o_coa, o_lat, o_conv = refs[6 + len(consts) : 12 + len(consts)]
    g = SimpleNamespace(**dict(zip(SCRATCH, refs[12 + len(consts) :])))
    r, c = lax.axis_index("rows"), lax.axis_index("cols")
    y, x_lo = r // 2, r % 2
    x_hi, z, core = c // 32, (c // 2) % 16, c % 2
    x = x_hi * 2 + x_lo
    z_hi, z_lo = z // 4, z % 4
    other = 1 - core
    e_n, e_s = 1 - (r + NR - 1) // NR, (r + 1) // NR
    e_w, e_e = 1 - (c + NC - 1) // NC, (c + 1) // NC
    variant = (e_n + 2 * e_s) * 3 + e_w + 2 * e_e

    up, down = (r + NR - 1) % NR, (r + 1) % NR
    left, right = (c + NC - 1) % NC, (c + 1) % NC

    def dev_x(d):
        t = (x + d) % 4
        return (y * 2 + t % 2, (t // 2) * 32 + z * 2 + core), t

    def dev_y(d):
        t = (y + d) % 4
        return (t * 2 + x_lo, c), t

    def dev_zlo(d):
        t = (z_lo + d) % 4
        return (r, x_hi * 32 + (z_hi * 4 + t) * 2 + core), t

    def dev_zhi(d, k):
        t = (z_hi + d) % 4
        return (r, x_hi * 32 + (t * 4 + z_lo) * 2 + k), t

    partner = (r, x_hi * 32 + z * 2 + other)

    loads = []

    def load(src, dst):
        copy = pltpu.make_async_copy(src, dst, g.lsem.at[len(loads)])
        copy.start()
        loads.append(copy)
        return copy

    inputs = [
        load(fin, g.finx.at[64:576]),
        load(mid, g.midx.at[32:160]),
        load(coa, g.coax.at[16:48]),
        load(coa, g.coab.at[0:32]),
        load(k.pf, g.v_pf),
        load(k.pm, g.v_pm),
        load(k.pc, g.v_pc),
    ]
    forward = [
        load(k.s1, g.v_s1),
        load(wl, g.v_wl),
        load(k.u1.at[variant], g.v_u1),
        load(k.u2.at[variant], g.v_u2),
    ]
    load_wo = load(wo_hbm, g.v_wo)
    load_cot = load(cot, g.v_cot)
    load_sf = load(k.sf, g.v_sf)
    backward = [
        load(k.d1.at[variant], g.v_d1),
        load(k.d2.at[variant], g.v_d2),
        load(k.pm0, g.v_pm0),
        load(k.sm, g.v_sm),
    ]

    def wait(copies):
        for copy in copies:
            copy.wait()

    peers = [(up, c), (down, c)] + [(a, b) for a in (r, up, down) for b in (left, right)]
    peers += [partner]
    for d in (1, 2, 3):
        peers += [dev_x(d)[0], dev_y(d)[0], dev_zlo(d)[0], dev_zhi(d, core)[0], dev_zhi(d, other)[0]]
    barrier = pltpu.get_barrier_semaphore()
    for p in peers:
        pl.semaphore_signal(barrier, inc=1, device_id=p, device_id_type=MESH)

    for ref, at, count in ((g.coab, 32, 96), (g.topb, 96, 32), (g.midb, 224, 32), (g.dfx, 672, 96), (g.dmx, 224, 32)):
        ref[at : at + count] = jnp.zeros((count, C), BF)
    for ref in (g.rs1, g.rs2, g.rs3, g.rs4):
        ref[96:128] = jnp.zeros((32, C), BF)

    used = [0]

    def send(src, dst, to):
        n = used[0]
        used[0] += 1
        copy = pltpu.make_async_remote_copy(
            src_ref=src,
            dst_ref=dst,
            send_sem=g.ssem.at[n],
            recv_sem=g.rsem.at[n],
            device_id=to,
            device_id_type=MESH,
        )
        copy.start()
        return copy

    sent = []

    def received(copies):
        for copy in copies:
            copy.wait_recv()
        sent.extend(copies)

    def send_rows(buf, h, w):
        return [
            send(buf.at[w : 2 * w], buf.at[w * (h + 1) : w * (h + 2)], (up, c)),
            send(buf.at[w * h : w * (h + 1)], buf.at[0:w], (down, c)),
        ]

    def send_sides(pack, slots):
        west, east = pack.at[0:16], pack.at[16:32]

        def slot(n):
            return slots.at[16 * n : 16 * n + 16]

        return [
            send(east, slot(0), (r, right)),
            send(east, slot(1), (down, right)),
            send(east, slot(2), (up, right)),
            send(west, slot(3), (r, left)),
            send(west, slot(4), (down, left)),
            send(west, slot(5), (up, left)),
        ]

    wait(inputs)
    packed = dot(g.v_pf[...], g.finx[64:576])
    packed += dot(g.v_pm[...], g.midx[32:160])
    packed += dot(g.v_pc[...], g.coab[...])
    g.pk1[...] = packed.astype(BF)
    pl.semaphore_wait(barrier, len(peers))
    halo = send_sides(g.pk1, g.rs1)
    halo += send_rows(g.coax, 2, 16)
    halo += send_rows(g.midx, 4, 32)
    halo += send_rows(g.finx, 8, 64)
    wait(forward)
    received(halo)
    sides = dot(g.v_s1[...], g.rs1[...]).astype(BF)
    g.finx[640:672] = sides[0:32]
    g.midx[192:224] = sides[32:64]
    g.coax[64:96] = sides[64:96]

    wl = g.v_wl
    w_fine, w_mid, w_top = wl[0:C], wl[C : 2 * C], wl[2 * C : 3 * C]
    g.topb[0:96] = dot(g.coax[0:96], w_top).astype(BF)
    g.midb[0:224] = (dot(g.midx[...], w_mid) + dot(g.v_u1[...], g.topb[...])).astype(BF)
    g.fex[...] = dot(g.finx[...], w_fine) + dot(g.v_u2[...], g.midb[...])

    keep_n, keep_s = (1 - e_n).astype(F32), (1 - e_s).astype(F32)
    keep_w, keep_e = (1 - e_w).astype(F32), (1 - e_e).astype(F32)
    line = lax.broadcasted_iota(jnp.int32, (16, C), 0)
    keep_rows = jnp.where(line == 0, keep_n, jnp.where(line == 9, keep_s, 1.0))

    def spread(north, body, south, west, east, out, flip):
        s = g.shift
        s[0, 8:72] = north * keep_n
        s[1:9, 8:72] = body.reshape(8, 64, C)
        s[9, 8:72] = south * keep_s
        west = west * (keep_rows * keep_w)
        east = east * (keep_rows * keep_e)
        for i in range(10):
            s[i, 7:8] = west[i : i + 1]
            s[i, 72:73] = east[i : i + 1]
        for b in range(3):
            at = 9 - b if flip else 7 + b
            out[:, b * C : (b + 1) * C] = s[:, at : at + 64].astype(BF).reshape(640, C)

    fex = g.fex
    spread(fex[0:64], fex[64:576], fex[576:640], fex[640:656], fex[656:672], g.fsh, False)

    load_wo.wait()
    wo, fsh, dsh = g.v_wo, g.fsh, g.dsh
    g.pre[...] = sum(dot(fsh[64 * a : 64 * a + 512], wo[768 * a : 768 * a + 768]) for a in range(3))
    load_cot.wait()

    def activate(q, carry):
        at = pl.multiple_of(q * 64, 64)
        v = g.pre[pl.ds(at, 64)]
        half = 0.5 + 0.5 * lax.erf(v * np.float32(np.sqrt(0.5)))
        g.maskb[pl.ds(at, 64)] = (v * half).astype(BF)
        slope = half + v * (jnp.exp(-0.5 * v * v) * np.float32(1 / np.sqrt(2 * np.pi)))
        g.dpx[pl.ds(at + 64, 64)] = (g.v_cot[pl.ds(at, 64)].astype(F32) * slope).astype(BF)
        return carry

    lax.fori_loop(0, 8, activate, 0)
    stores = []

    def store(src, dst):
        copy = pltpu.make_async_copy(src, dst, g.osem.at[len(stores)])
        copy.start()
        stores.append(copy)

    store(g.maskb, o_mask)

    load_sf.wait()
    halo = send_rows(g.dpx, 8, 64)
    g.pk2[...] = dot(g.v_pf[...], g.dpx[64:576]).astype(BF)
    halo += send_sides(g.pk2, g.rs2)

    grad, got = g.grad, g.got
    dpre_t = g.dpx[64:576].T
    pair = []
    for a in range(3):
        lanes = pl.ds(768 * a, 768)
        term = dot(dpre_t, fsh[64 * a : 64 * a + 512]).astype(BF)
        grad[:, :, :, lanes] = term.reshape(8, 2, 16, 768)
        pair.append(send(grad.at[:, other, :, lanes], got.at[:, :, lanes], partner))

    received(halo)
    sides = dot(g.v_sf[...], g.rs2[...])
    dpx = g.dpx
    spread(
        dpx[0:64].astype(F32), dpx[64:576].astype(F32), dpx[576:640].astype(F32),
        sides[0:16], sides[16:32], dsh, True,
    )
    dfine = None
    for a in range(3):
        for b in range(3):
            t = 3 * a + b
            term = dot_t(dsh[64 * (2 - a) : 64 * (2 - a) + 512, b * C : (b + 1) * C], wo[t * C : (t + 1) * C])
            dfine = term if dfine is None else dfine + term
    dfx = g.dfx
    dfx[64:576] = dfine.astype(BF)
    halo = send_rows(dfx, 8, 64)
    g.pk3[...] = dot(g.v_pf[...], dfx[64:576]).astype(BF)
    halo += send_sides(g.pk3, g.rs3)

    def begin(buf, slots, dev):
        out = []
        for d in (1, 2, 3):
            to, t = dev(d)
            out.append(send(buf.at[t], slots.at[d - 1], to))
        return out

    def total(buf, mine, slots):
        return buf[mine].astype(F32) + slots[0].astype(F32) + slots[1].astype(F32) + slots[2].astype(F32)

    def split(mine, theirs, half, first, p, q):
        wp, wq = p.shape[-1], q.shape[-1]
        for n in range(8):
            part = (mine[n, core].astype(F32) + theirs[n].astype(F32)).astype(BF)
            for h in range(2):
                at = half * h
                p[2 * h + n % 2, n // 2] = part[:, at : at + wp]
                q[n // 2, 2 * h + n % 2] = part[:, at + wp : at + wp + wq]

    received(pair)
    split(grad, got, 1152, 0, g.cp1, g.cq1)
    cp = begin(g.cp1, g.cp1r, dev_x)
    cq = begin(g.cq1, g.cq1r, dev_y)

    g.fgb[...] = dot_t(dfx[64:576], w_fine).astype(BF)
    store(g.fgb, o_fine)
    lgrad, lgot = g.lgrad, g.lgot
    lgrad[:, :, :, 0:C] = dot(dfx[64:576].T, g.finx[64:576]).astype(BF).reshape(8, 2, 16, C)
    lpair = [send(lgrad.at[:, other, :, pl.ds(0, C)], lgot.at[:, :, pl.ds(0, C)], partner)]

    received(halo)
    wait(backward)
    dfx[640:672] = dot(g.v_sf[...], g.rs3[...]).astype(BF)
    dmx = g.dmx
    dmx[32:160] = dot(g.v_d1[...], dfx[...]).astype(BF)
    halo = send_rows(dmx, 4, 32)
    g.pk4[...] = dot(g.v_pm0[...], dmx[32:160]).astype(BF)
    halo += send_sides(g.pk4, g.rs4)

    received(cp)
    g.cp2[...] = total(g.cp1, x, g.cp1r).astype(BF)
    cp = begin(g.cp2, g.cp2r, dev_y)
    received(cq)
    g.cq2[...] = total(g.cq1, y, g.cq1r).astype(BF)
    cq = begin(g.cq2, g.cq2r, dev_x)

    g.mgb[...] = dot_t(dmx[32:160], w_mid).astype(BF)
    store(g.mgb, o_mid)
    lgrad[:, :, :, C : 2 * C] = dot(dmx[32:160].T, g.midx[32:160]).astype(BF).reshape(8, 2, 16, C)
    lpair += [send(lgrad.at[:, other, :, pl.ds(C, C)], lgot.at[:, :, pl.ds(C, C)], partner)]

    received(halo)
    dmx[192:224] = dot(g.v_sm[...], g.rs4[...]).astype(BF)
    dtop = dot(g.v_d2[...], dmx[...]).astype(BF)
    g.cgb[...] = dot_t(dtop[0:32], w_top).astype(BF)
    store(g.cgb, o_coa)
    lgrad[:, :, :, 2 * C : 3 * C] = dot(dtop.T, g.coab[...]).astype(BF).reshape(8, 2, 16, C)
    lpair += [send(lgrad.at[:, other, :, pl.ds(2 * C, C)], lgot.at[:, :, pl.ds(2 * C, C)], partner)]

    received(lpair)
    split(lgrad, lgot, 384, 0, g.lp1, g.lq1)
    lp = begin(g.lp1, g.lp1r, dev_x)
    lq = begin(g.lq1, g.lq1r, dev_y)
    sums = g.sums
    received(cp)
    sums[:, 0:CP] = total(g.cp2, y, g.cp2r)
    received(cq)
    sums[:, CP : CP + CQ] = total(g.cq2, x, g.cq2r)
    received(lp)
    g.lp2[...] = total(g.lp1, x, g.lp1r).astype(BF)
    lp = begin(g.lp2, g.lp2r, dev_y)
    received(lq)
    g.lq2[...] = total(g.lq1, y, g.lq1r).astype(BF)
    lq = begin(g.lq2, g.lq2r, dev_x)
    received(lp)
    sums[:, 1152 : 1152 + LP] = total(g.lp2, y, g.lp2r)
    received(lq)
    sums[:, 1152 + LP : 1536] = total(g.lq2, x, g.lq2r)

    lane = lax.broadcasted_iota(jnp.int32, (16, LANE), 1)

    def window(base, count, start):
        t, off = start // LANE, start % LANE

        def tile(n):
            n = min(max(n, 0), count // LANE - 1)
            return sums[:, base + n * LANE : base + (n + 1) * LANE]

        if off == 0:
            return tile(t)
        return jnp.where(
            lane < LANE - off,
            pltpu.roll(tile(t), LANE - off, 1),
            pltpu.roll(tile(t + 1), LANE - off, 1),
        )

    for n in range(16):
        conv = window(0, 1152, 72 * n)
        lat = window(1152, 384, 24 * n - 72)
        g.z1[n % 4, n // 4] = jnp.where(lane < 72, conv, lat).astype(BF)
    zc = begin(g.z1, g.z1r, dev_zlo)
    received(zc)
    g.z2[...] = total(g.z1, z_lo, g.z1r).astype(BF)
    z2, fin = g.z2, g.fin_r
    zc = [send(z2.at[z_hi], fin.at[1, 0], partner)]
    for d in (1, 2, 3):
        for e, k in ((0, core), (1, other)):
            to, t = dev_zhi(d, k)
            zc.append(send(z2.at[t], fin.at[e, d], to))
    received(zc)
    same = z2[z_hi].astype(F32) + sum(fin[0, d].astype(F32) for d in (1, 2, 3))
    cross = sum(fin[1, d].astype(F32) for d in range(4))
    first = core == 0
    rows32 = [jnp.where(first, same, cross), jnp.where(first, cross, same)]
    g.turn[...] = jnp.concatenate(rows32 + [jnp.zeros((96, LANE), F32)], 0).T
    turn = g.turn
    o_conv[...] = jnp.where(first, turn[0:36, 0:32], turn[36:72, 0:32])
    o_lat[...] = jnp.where(first, turn[72:84, 0:32], turn[84:96, 0:32])

    for copy in sent:
        copy.wait_send()
    wait(stores)


VM = pltpu.VMEM
DMA = pltpu.SemaphoreType.DMA
SCRATCH = dict(
    finx=VM((672, C), BF),
    midx=VM((224, C), BF),
    coax=VM((96, C), BF),
    coab=VM((128, C), BF),
    v_wl=VM((768, C), BF),
    v_wo=VM((2304, C), BF),
    v_cot=VM((512, C), BF),
    v_u1=VM((224, 128), BF),
    v_u2=VM((672, 256), BF),
    v_d1=VM((128, 768), BF),
    v_d2=VM((128, 256), BF),
    v_pf=VM((32, 512), BF),
    v_pm=VM((32, 128), BF),
    v_pc=VM((32, 128), BF),
    v_pm0=VM((32, 128), BF),
    v_s1=VM((96, 128), BF),
    v_sf=VM((32, 128), BF),
    v_sm=VM((32, 128), BF),
    topb=VM((128, C), BF),
    midb=VM((256, C), BF),
    fex=VM((672, C), F32),
    shift=VM((10, 80, C), F32),
    fsh=VM((640, 768), BF),
    dsh=VM((640, 768), BF),
    pre=VM((512, C), F32),
    maskb=VM((512, C), BF),
    dpx=VM((640, C), BF),
    dfx=VM((768, C), BF),
    dmx=VM((256, C), BF),
    fgb=VM((512, C), BF),
    mgb=VM((128, C), BF),
    cgb=VM((32, C), BF),
    pk1=VM((32, C), BF),
    pk2=VM((32, C), BF),
    pk3=VM((32, C), BF),
    pk4=VM((32, C), BF),
    rs1=VM((128, C), BF),
    rs2=VM((128, C), BF),
    rs3=VM((128, C), BF),
    rs4=VM((128, C), BF),
    grad=VM((8, 2, 16, 2304), BF),
    got=VM((8, 16, 2304), BF),
    lgrad=VM((8, 2, 16, 768), BF),
    lgot=VM((8, 16, 768), BF),
    cp1=VM((4, 4, 16, CP), BF),
    cp1r=VM((3, 4, 16, CP), BF),
    cp2=VM((4, 16, CP), BF),
    cp2r=VM((3, 16, CP), BF),
    cq1=VM((4, 4, 16, CQ), BF),
    cq1r=VM((3, 4, 16, CQ), BF),
    cq2=VM((4, 16, CQ), BF),
    cq2r=VM((3, 16, CQ), BF),
    lp1=VM((4, 4, 16, LP), BF),
    lp1r=VM((3, 4, 16, LP), BF),
    lp2=VM((4, 16, LP), BF),
    lp2r=VM((3, 16, LP), BF),
    lq1=VM((4, 4, 16, LQ), BF),
    lq1r=VM((3, 4, 16, LQ), BF),
    lq2=VM((4, 16, LQ), BF),
    lq2r=VM((3, 16, LQ), BF),
    sums=VM((16, 1536), F32),
    z1=VM((4, 4, 16, LANE), BF),
    z1r=VM((3, 4, 16, LANE), BF),
    z2=VM((4, 16, LANE), BF),
    fin_r=VM((2, 4, 16, LANE), BF),
    turn=VM((128, 128), F32),
    lsem=DMA((20,)),
    osem=DMA((4,)),
    ssem=DMA((80,)),
    rsem=DMA((80,)),
)


def local(consts, fine_in, mid_in, coarse_in, lateral_weight, out_weight, cotangent):
    def flat(v):
        return v.reshape(-1, v.shape[-1])

    args = [flat(fine_in), flat(mid_in), flat(coarse_in), lateral_weight, out_weight, flat(cotangent)]
    args += [jnp.asarray(v) for v in consts.values()]
    hbm = pl.BlockSpec(memory_space=pl.ANY)
    vmem = pl.BlockSpec(memory_space=pltpu.VMEM)
    outs = pl.pallas_call(
        functools.partial(kernel, tuple(consts)),
        out_shape=[
            jax.ShapeDtypeStruct((512, C), BF),
            jax.ShapeDtypeStruct((512, C), BF),
            jax.ShapeDtypeStruct((128, C), BF),
            jax.ShapeDtypeStruct((32, C), BF),
            jax.ShapeDtypeStruct((12, 32), F32),
            jax.ShapeDtypeStruct((36, 32), F32),
        ],
        in_specs=[hbm] * len(args),
        out_specs=[hbm] * 4 + [vmem] * 2,
        scratch_shapes=list(SCRATCH.values()),
        compiler_params=pltpu.CompilerParams(
            collective_id=0, has_side_effects=True, vmem_limit_bytes=40 * 2**20
        ),
        cost_estimate=pl.CostEstimate(flops=2_400_000_000, bytes_accessed=4_000_000, transcendentals=262144),
    )(*args)
    return (
        outs[0].reshape(fine_in.shape),
        outs[1].reshape(fine_in.shape),
        outs[2].reshape(mid_in.shape),
        outs[3].reshape(coarse_in.shape),
        outs[4],
        outs[5],
    )


def solution(mesh):
    field = P("rows", "cols", None)
    return jax.shard_map(
        functools.partial(local, constants()),
        mesh=mesh,
        in_specs=(field, field, field, P(), P(), field),
        out_specs=(field, field, field, field, P("cols", "rows"), P("cols", "rows")),
        check_vma=False,
    )
```

```python
import functools
from types import SimpleNamespace

import jax
import jax.numpy as jnp
import ml_dtypes
import numpy as np
from jax import lax
from jax.experimental import pallas as pl
from jax.experimental.pallas import tpu as pltpu
from jax.sharding import PartitionSpec as P

BF = jnp.bfloat16
F32 = jnp.float32
MESH = pl.DeviceIdType.MESH
C = 256
NR, NC = 8, 64
LANE = 128


def place(h, w, i, j):
    if j < 0:
        return w * (h + 2) + i + 1
    if j >= w:
        return w * (h + 2) + 16 + i + 1
    return (i + 1) * w + j


def size(h, w):
    return w * (h + 2) + 32


def cells(h, w):
    return [(i, j) for i in range(-1, h + 1) for j in range(-1, w + 1)]


def clamp(i, n, kind):
    if kind == 1:
        i = max(i, 0)
    if kind == 2:
        i = min(i, n - 1)
    return i


def up_taps(i):
    k = i // 2
    if i % 2 == 0:
        return [(k - 1, 0.25), (k, 0.75)]
    return [(k, 0.75), (k + 1, 0.25)]


def up_matrix(h, w, pad):
    mat = np.zeros((9, size(2 * h, 2 * w), pad), np.float32)
    for v in range(9):
        for i, j in cells(2 * h, 2 * w):
            for ri, rw in up_taps(i):
                for ci, cw in up_taps(j):
                    ri2, ci2 = clamp(ri, h, v // 3), clamp(ci, w, v % 3)
                    mat[v, place(2 * h, 2 * w, i, j), place(h, w, ri2, ci2)] += rw * cw
    return mat.astype(ml_dtypes.bfloat16)


def down_matrix(h, w, rows, pad):
    mat = np.zeros((9, rows, pad), np.float32)
    weights = (0.25, 0.75, 0.75, 0.25)
    for v in range(9):
        for i in range(h):
            for j in range(w):
                for a in range(4):
                    for b in range(4):
                        ri = clamp(2 * i - 1 + a, 2 * h, v // 3)
                        ci = clamp(2 * j - 1 + b, 2 * w, v % 3)
                        mat[v, i * w + j, place(2 * h, 2 * w, ri, ci)] += weights[a] * weights[b]
    return mat.astype(ml_dtypes.bfloat16)


def down_line(n, kind):
    line = np.zeros((n + 2, 2 * n + 4))
    for k in range(-1, n + 1):
        if (kind == 1 and k < 0) or (kind == 2 and k >= n):
            continue
        for a, weight in enumerate((0.25, 0.75, 0.75, 0.25)):
            f = clamp(2 * k - 1 + a, 2 * n, kind)
            if -2 <= f < 2 * n + 2:
                line[k + 1, f + 2] += weight
    return line


def adjoint_matrix(h, w, steps, pad):
    fh, fw = h << steps, w << steps
    mat = np.zeros((9, fh * fw, pad), np.float32)
    for v in range(9):
        lines = []
        for n, kind in ((h, v // 3), (w, v % 3)):
            line = down_line(n, kind)
            for s in range(1, steps):
                line = line[:, 1:-1] @ down_line(n << s, kind)
            lines.append(line[:, 2:-2])
        both = np.multiply.outer(*lines)
        for i in range(-1, h + 1):
            for j in range(-1, w + 1):
                mat[v, :, place(h, w, i, j)] = both[i + 1, :, j + 1, :].reshape(-1)
    return mat.astype(ml_dtypes.bfloat16)


def pack_matrix(h, w, first, cols):
    mat = np.zeros((32, cols), np.float32)
    for i in range(h):
        mat[first + i, i * w] = 1
        mat[16 + first + i, i * w + w - 1] = 1
    return mat.astype(ml_dtypes.bfloat16)


def side_matrix(levels):
    mat = np.zeros((32 * len(levels), LANE), np.float32)
    for n, (h, first) in enumerate(levels):
        for side in range(2):
            row, src = 32 * n + 16 * side, 48 * side
            mat[row, src + 16 + first + h - 1] = 1
            for i in range(h):
                mat[row + 1 + i, src + first + i] = 1
            mat[row + 1 + h, src + 32 + first] = 1
    return mat.astype(ml_dtypes.bfloat16)


def constants():
    packs = [
        pack_matrix(8, 64, 0, 512),
        pack_matrix(4, 32, 8, 128),
        pack_matrix(2, 16, 12, 32),
        pack_matrix(4, 32, 0, 128),
    ]
    return dict(
        u1=up_matrix(2, 16, 128),
        u2=up_matrix(4, 32, 256),
        d1=down_matrix(4, 32, 128, 768),
        d2=down_matrix(2, 16, 128, 256),
        a1=adjoint_matrix(4, 32, 1, 256),
        a2=adjoint_matrix(2, 16, 2, 128),
        pf=packs[0],
        pm=packs[1],
        pc=np.concatenate([packs[2], np.zeros((32, 96), ml_dtypes.bfloat16)], 1),
        pm0=packs[3],
        s1=side_matrix([(8, 0), (4, 8), (2, 12)]),
        sf=side_matrix([(8, 0)]),
        sm=side_matrix([(4, 0)]),
    )


CP, CQ, LP, LQ = 640, 512, 128, 256


def dot(a, b):
    return jnp.dot(a, b, preferred_element_type=F32)


def dot_t(a, b):
    return lax.dot_general(a, b, (((1,), (1,)), ((), ())), preferred_element_type=F32)


def kernel(consts, *refs):
    fin, mid, coa, wl, wo_hbm, cot = refs[:6]
    k = SimpleNamespace(**dict(zip(consts, refs[6 : 6 + len(consts)])))
    o_mask, o_fine, o_mid, o_coa, o_lat, o_conv = refs[6 + len(consts) : 12 + len(consts)]
    g = SimpleNamespace(**dict(zip(SCRATCH, refs[12 + len(consts) :])))
    r, c = lax.axis_index("rows"), lax.axis_index("cols")
    y, x_lo = r // 2, r % 2
    x_hi, z, core = c // 32, (c // 2) % 16, c % 2
    x = x_hi * 2 + x_lo
    other = 1 - core
    e_n, e_s = 1 - (r + NR - 1) // NR, (r + 1) // NR
    e_w, e_e = 1 - (c + NC - 1) // NC, (c + 1) // NC
    variant = (e_n + 2 * e_s) * 3 + e_w + 2 * e_e

    up, down = (r + NR - 1) % NR, (r + 1) % NR
    left, right = (c + NC - 1) % NC, (c + 1) % NC

    def dev_x(d):
        t = (x + d) % 4
        return (y * 2 + t % 2, (t // 2) * 32 + z * 2 + core), t

    def dev_y(d):
        t = (y + d) % 4
        return (t * 2 + x_lo, c), t

    def dev_z(d):
        t = (z + d) % 16
        return (r, x_hi * 32 + t * 2 + core), t

    partner = (r, x_hi * 32 + z * 2 + other)

    loads = []

    def load(src, dst):
        copy = pltpu.make_async_copy(src, dst, g.lsem.at[len(loads)])
        copy.start()
        loads.append(copy)
        return copy

    inputs = [
        load(fin, g.finx.at[64:576]),
        load(mid, g.midx.at[32:160]),
        load(coa, g.coax.at[16:48]),
        load(coa, g.coab.at[0:32]),
        load(k.pf, g.v_pf),
        load(k.pm, g.v_pm),
        load(k.pc, g.v_pc),
    ]
    forward = [
        load(k.s1, g.v_s1),
        load(wl, g.v_wl),
        load(k.u1.at[variant], g.v_u1),
        load(k.u2.at[variant], g.v_u2),
        load(k.a1.at[variant], g.v_a1),
        load(k.a2.at[variant], g.v_a2),
    ]
    load_wo = load(wo_hbm, g.v_wo)
    load_cot = load(cot, g.v_cot)
    load_sf = load(k.sf, g.v_sf)
    backward = [
        load(k.d1.at[variant], g.v_d1),
        load(k.d2.at[variant], g.v_d2),
        load(k.pm0, g.v_pm0),
        load(k.sm, g.v_sm),
    ]

    def wait(copies):
        for copy in copies:
            copy.wait()

    peers = [(up, c), (down, c)] + [(a, b) for a in (r, up, down) for b in (left, right)]
    for d in (1, 2, 3):
        peers += [dev_x(d)[0], dev_y(d)[0]]
    peers += [dev_z(1)[0], dev_z(15)[0]]
    barrier = pltpu.get_barrier_semaphore()
    for p in peers:
        pl.semaphore_signal(barrier, inc=1, device_id=p, device_id_type=MESH)

    def greet(n):
        for d in (1 << n, 16 - (1 << n)):
            pl.semaphore_signal(g.far.at[n], inc=1, device_id=dev_z(d)[0], device_id_type=MESH)

    def met(n):
        pl.semaphore_wait(g.far.at[n], 2)

    for ref, at, count in ((g.coab, 32, 96), (g.midx, 224, 32), (g.coax, 96, 32), (g.topb, 96, 32), (g.midb, 224, 32), (g.dfx, 672, 96), (g.dmx, 224, 32)):
        ref[at : at + count] = jnp.zeros((count, C), BF)
    for ref in (g.rs1, g.rs2, g.rs3, g.rs4):
        ref[96:128] = jnp.zeros((32, C), BF)

    used = [0]

    def send(src, dst, to):
        n = used[0]
        used[0] += 1
        copy = pltpu.make_async_remote_copy(
            src_ref=src,
            dst_ref=dst,
            send_sem=g.ssem.at[n],
            recv_sem=g.rsem.at[n],
            device_id=to,
            device_id_type=MESH,
        )
        copy.start()
        return copy

    sent = []

    def received(copies):
        for copy in copies:
            copy.wait_recv()
        sent.extend(copies)

    def send_rows(buf, h, w):
        return [
            send(buf.at[w : 2 * w], buf.at[w * (h + 1) : w * (h + 2)], (up, c)),
            send(buf.at[w * h : w * (h + 1)], buf.at[0:w], (down, c)),
        ]

    def send_sides(pack, slots):
        west, east = pack.at[0:16], pack.at[16:32]

        def slot(n):
            return slots.at[16 * n : 16 * n + 16]

        return [
            send(east, slot(0), (r, right)),
            send(east, slot(1), (down, right)),
            send(east, slot(2), (up, right)),
            send(west, slot(3), (r, left)),
            send(west, slot(4), (down, left)),
            send(west, slot(5), (up, left)),
        ]

    wait(inputs)
    packed = dot(g.v_pf[...], g.finx[64:576])
    packed += dot(g.v_pm[...], g.midx[32:160])
    packed += dot(g.v_pc[...], g.coab[...])
    g.pk1[...] = packed.astype(BF)
    pl.semaphore_wait(barrier, len(peers))
    halo = send_sides(g.pk1, g.rs1)
    halo += send_rows(g.coax, 2, 16)
    halo += send_rows(g.midx, 4, 32)
    halo += send_rows(g.finx, 8, 64)
    greet(0)
    wait(forward)
    wl = g.v_wl
    w_fine, w_mid, w_top = wl[0:C], wl[C : 2 * C], wl[2 * C : 3 * C]
    fex = g.fex
    fex[64:576] = dot(g.finx[64:576], w_fine)
    received(halo)
    met(0)
    greet(1)
    sides = dot(g.v_s1[...], g.rs1[...]).astype(BF)
    g.finx[640:672] = sides[0:32]
    g.midx[192:224] = sides[32:64]
    g.coax[64:96] = sides[64:96]

    g.topb[0:96] = dot(g.coax[0:96], w_top).astype(BF)
    g.midb[0:224] = (dot(g.midx[0:224], w_mid) + dot(g.v_u1[...], g.topb[...])).astype(BF)
    fex[0:64] = dot(g.finx[0:64], w_fine)
    fex[576:672] = dot(g.finx[576:672], w_fine)
    fex[...] += dot(g.v_u2[...], g.midb[...])

    keep_n, keep_s = (1 - e_n).astype(F32), (1 - e_s).astype(F32)
    keep_w, keep_e = (1 - e_w).astype(F32), (1 - e_e).astype(F32)
    line = lax.broadcasted_iota(jnp.int32, (16, C), 0)
    keep_rows = jnp.where(line == 0, keep_n, jnp.where(line == 9, keep_s, 1.0))

    def spread(north, body, south, west, east, out, flip):
        s = g.shift
        s[0, 8:72] = north * keep_n
        s[1:9, 8:72] = body.reshape(8, 64, C)
        s[9, 8:72] = south * keep_s
        west = west * (keep_rows * keep_w)
        east = east * (keep_rows * keep_e)
        for i in range(10):
            s[i, 7:8] = west[i : i + 1]
            s[i, 72:73] = east[i : i + 1]
        for b in range(3):
            at = 9 - b if flip else 7 + b
            out[:, b * C : (b + 1) * C] = s[:, at : at + 64].astype(BF).reshape(640, C)

    spread(fex[0:64], fex[64:576], fex[576:640], fex[640:656], fex[656:672], g.fsh, False)

    load_wo.wait()
    wo, fsh, dsh = g.v_wo, g.fsh, g.dsh
    g.pre[...] = sum(dot(fsh[64 * a : 64 * a + 512], wo[768 * a : 768 * a + 768]) for a in range(3))
    load_cot.wait()

    def activate(q, carry):
        at = pl.multiple_of(q * 64, 64)
        v = g.pre[pl.ds(at, 64)]
        half = 0.5 + 0.5 * lax.erf(v * np.float32(np.sqrt(0.5)))
        g.maskb[pl.ds(at, 64)] = (v * half).astype(BF)
        slope = half + v * (jnp.exp(-0.5 * v * v) * np.float32(1 / np.sqrt(2 * np.pi)))
        g.dpx[pl.ds(at + 64, 64)] = (g.v_cot[pl.ds(at, 64)].astype(F32) * slope).astype(BF)
        return carry

    lax.fori_loop(0, 8, activate, 0)
    g.xm[...] = dot(g.v_a1[...], g.midx[...]).astype(BF)
    g.xc[...] = dot(g.v_a2[...], g.coax[...]).astype(BF)
    stores = []

    def store(src, dst):
        copy = pltpu.make_async_copy(src, dst, g.osem.at[len(stores)])
        copy.start()
        stores.append(copy)

    store(g.maskb, o_mask)

    load_sf.wait()
    halo = send_rows(g.dpx, 8, 64)
    g.pk2[...] = dot(g.v_pf[...], g.dpx[64:576]).astype(BF)
    halo += send_sides(g.pk2, g.rs2)

    grad, got = g.grad, g.got
    dpre_t = g.dpx[64:576].T
    pair = []
    for a in range(3):
        lanes = pl.ds(768 * a, 768)
        term = dot(dpre_t, fsh[64 * a : 64 * a + 512]).astype(BF)
        grad[:, :, :, lanes] = term.reshape(8, 2, 16, 768)
        pair.append(send(grad.at[:, other, :, lanes], got.at[:, :, lanes], partner))

    def begin(buf, slots, dev):
        out = []
        for d in (1, 2, 3):
            to, t = dev(d)
            out.append(send(buf.at[t], slots.at[d - 1], to))
        return out

    def total(buf, mine, slots):
        return buf[mine].astype(F32) + slots[0].astype(F32) + slots[1].astype(F32) + slots[2].astype(F32)

    def split(mine, theirs, half, first, p, q):
        wp, wq = p.shape[-1], q.shape[-1]
        for n in range(8):
            part = (mine[n, core].astype(F32) + theirs[n].astype(F32)).astype(BF)
            for h in range(2):
                at = half * h
                p[2 * h + n % 2, n // 2] = part[:, at : at + wp]
                q[n // 2, 2 * h + n % 2] = part[:, at + wp : at + wp + wq]

    received(pair)
    split(grad, got, 1152, 0, g.cp1, g.cq1)
    cp = begin(g.cp1, g.cp1r, dev_x)
    cq = begin(g.cq1, g.cq1r, dev_y)
    met(1)
    greet(2)

    received(halo)
    sides = dot(g.v_sf[...], g.rs2[...])
    dpx = g.dpx
    spread(
        dpx[0:64].astype(F32), dpx[64:576].astype(F32), dpx[576:640].astype(F32),
        sides[0:16], sides[16:32], dsh, True,
    )
    dfine = None
    for a in range(3):
        for b in range(3):
            t = 3 * a + b
            term = dot_t(dsh[64 * (2 - a) : 64 * (2 - a) + 512, b * C : (b + 1) * C], wo[t * C : (t + 1) * C])
            dfine = term if dfine is None else dfine + term
    dfx = g.dfx
    dfx[64:576] = dfine.astype(BF)

    lgrad, lgot = g.lgrad, g.lgot
    dfine_t = dfx[64:576].T
    lpair = []
    for n, rows in enumerate((g.finx[64:576], g.xm[...], g.xc[...])):
        lanes = pl.ds(n * C, C)
        lgrad[:, :, :, lanes] = dot(dfine_t, rows).astype(BF).reshape(8, 2, 16, C)
        lpair.append(send(lgrad.at[:, other, :, lanes], lgot.at[:, :, lanes], partner))
    halo = send_rows(dfx, 8, 64)
    g.pk3[...] = dot(g.v_pf[...], dfx[64:576]).astype(BF)
    halo += send_sides(g.pk3, g.rs3)

    received(lpair)
    split(lgrad, lgot, 384, 0, g.lp1, g.lq1)
    lp = begin(g.lp1, g.lp1r, dev_x)
    lq = begin(g.lq1, g.lq1r, dev_y)

    received(cp)
    g.cp2[...] = total(g.cp1, x, g.cp1r).astype(BF)
    cp = begin(g.cp2, g.cp2r, dev_y)
    received(cq)
    g.cq2[...] = total(g.cq1, y, g.cq1r).astype(BF)
    cq = begin(g.cq2, g.cq2r, dev_x)

    received(lp)
    g.lp2[...] = total(g.lp1, x, g.lp1r).astype(BF)
    lp = begin(g.lp2, g.lp2r, dev_y)
    received(lq)
    g.lq2[...] = total(g.lq1, y, g.lq1r).astype(BF)
    lq = begin(g.lq2, g.lq2r, dev_x)

    received(halo)
    wait(backward)
    dfx[640:672] = dot(g.v_sf[...], g.rs3[...]).astype(BF)
    dmx = g.dmx
    dmx[32:160] = dot(g.v_d1[...], dfx[...]).astype(BF)
    halo = send_rows(dmx, 4, 32)
    g.pk4[...] = dot(g.v_pm0[...], dmx[32:160]).astype(BF)
    halo += send_sides(g.pk4, g.rs4)

    sums = g.sums
    received(cp)
    sums[:, 0:CP] = total(g.cp2, y, g.cp2r)
    received(cq)
    sums[:, CP : CP + CQ] = total(g.cq2, x, g.cq2r)
    received(lp)
    sums[:, 1152 : 1152 + LP] = total(g.lp2, y, g.lp2r)
    received(lq)
    sums[:, 1152 + LP : 1536] = total(g.lq2, x, g.lq2r)

    lane = lax.broadcasted_iota(jnp.int32, (16, LANE), 1)

    def window(base, count, start):
        t, off = start // LANE, start % LANE

        def tile(n):
            n = min(max(n, 0), count // LANE - 1)
            return sums[:, base + n * LANE : base + (n + 1) * LANE]

        if off == 0:
            return tile(t)
        return jnp.where(
            lane < LANE - off,
            pltpu.roll(tile(t), LANE - off, 1),
            pltpu.roll(tile(t + 1), LANE - off, 1),
        )

    for n in range(16):
        conv = window(0, 1152, 72 * n)
        lat = window(1152, 384, 24 * n - 72)
        g.z1[n] = jnp.where(lane < 72, conv, lat).astype(BF)
    met(2)
    zc = []
    for d in range(1, 16):
        to, t = dev_z(d)
        zc.append(send(g.z1.at[t], g.z1r.at[d - 1], to))

    g.fgb[...] = dot_t(dfx[64:576], w_fine).astype(BF)
    store(g.fgb, o_fine)
    g.mgb[...] = dot_t(dmx[32:160], w_mid).astype(BF)
    store(g.mgb, o_mid)
    received(halo)
    dmx[192:224] = dot(g.v_sm[...], g.rs4[...]).astype(BF)
    dtop = dot(g.v_d2[...], dmx[...]).astype(BF)
    g.cgb[...] = dot_t(dtop[0:32], w_top).astype(BF)
    store(g.cgb, o_coa)

    received(zc)
    same = g.z1[z].astype(F32)
    for d in range(15):
        same += g.z1r[d].astype(F32)
    g.z2[...] = same.astype(BF)
    received([send(g.z2, g.z2r, partner)])
    cross = g.z2r[...].astype(F32)
    first = core == 0
    both = jnp.concatenate([jnp.where(first, same, cross), jnp.where(first, cross, same)], 0)
    o_conv[...] = jnp.where(first, both[:, 0:36], pltpu.roll(both, LANE - 36, 1)[:, 0:36])
    g.turn[...] = jnp.concatenate([both, jnp.zeros((96, LANE), F32)], 0).T
    o_lat[...] = jnp.where(first, g.turn[72:84, 0:32], g.turn[84:96, 0:32])

    for copy in sent:
        copy.wait_send()
    wait(stores)


VM = pltpu.VMEM
DMA = pltpu.SemaphoreType.DMA
SCRATCH = dict(
    finx=VM((672, C), BF),
    midx=VM((256, C), BF),
    coax=VM((128, C), BF),
    coab=VM((128, C), BF),
    v_wl=VM((768, C), BF),
    v_wo=VM((2304, C), BF),
    v_cot=VM((512, C), BF),
    v_u1=VM((224, 128), BF),
    v_u2=VM((672, 256), BF),
    v_d1=VM((128, 768), BF),
    v_d2=VM((128, 256), BF),
    v_pf=VM((32, 512), BF),
    v_pm=VM((32, 128), BF),
    v_pc=VM((32, 128), BF),
    v_pm0=VM((32, 128), BF),
    v_s1=VM((96, 128), BF),
    v_sf=VM((32, 128), BF),
    v_sm=VM((32, 128), BF),
    topb=VM((128, C), BF),
    midb=VM((256, C), BF),
    fex=VM((672, C), F32),
    shift=VM((10, 80, C), F32),
    fsh=VM((640, 768), BF),
    dsh=VM((640, 768), BF),
    pre=VM((512, C), F32),
    maskb=VM((512, C), BF),
    dpx=VM((640, C), BF),
    dfx=VM((768, C), BF),
    dmx=VM((256, C), BF),
    fgb=VM((512, C), BF),
    mgb=VM((128, C), BF),
    cgb=VM((32, C), BF),
    pk1=VM((32, C), BF),
    pk2=VM((32, C), BF),
    pk3=VM((32, C), BF),
    pk4=VM((32, C), BF),
    rs1=VM((128, C), BF),
    rs2=VM((128, C), BF),
    rs3=VM((128, C), BF),
    rs4=VM((128, C), BF),
    grad=VM((8, 2, 16, 2304), BF),
    got=VM((8, 16, 2304), BF),
    lgrad=VM((8, 2, 16, 768), BF),
    lgot=VM((8, 16, 768), BF),
    cp1=VM((4, 4, 16, CP), BF),
    cp1r=VM((3, 4, 16, CP), BF),
    cp2=VM((4, 16, CP), BF),
    cp2r=VM((3, 16, CP), BF),
    cq1=VM((4, 4, 16, CQ), BF),
    cq1r=VM((3, 4, 16, CQ), BF),
    cq2=VM((4, 16, CQ), BF),
    cq2r=VM((3, 16, CQ), BF),
    lp1=VM((4, 4, 16, LP), BF),
    lp1r=VM((3, 4, 16, LP), BF),
    lp2=VM((4, 16, LP), BF),
    lp2r=VM((3, 16, LP), BF),
    lq1=VM((4, 4, 16, LQ), BF),
    lq1r=VM((3, 4, 16, LQ), BF),
    lq2=VM((4, 16, LQ), BF),
    lq2r=VM((3, 16, LQ), BF),
    sums=VM((16, 1536), F32),
    z1=VM((16, 16, LANE), BF),
    z1r=VM((15, 16, LANE), BF),
    z2=VM((16, LANE), BF),
    z2r=VM((16, LANE), BF),
    far=pltpu.SemaphoreType.REGULAR((3,)),
    v_a1=VM((512, 256), BF),
    v_a2=VM((512, 128), BF),
    xm=VM((512, C), BF),
    xc=VM((512, C), BF),
    turn=VM((128, 128), F32),
    lsem=DMA((24,)),
    osem=DMA((4,)),
    ssem=DMA((96,)),
    rsem=DMA((96,)),
)


def hand_on(*refs):
    n = len(refs) // 2
    copies = [pltpu.make_async_copy(refs[i], refs[n + i], refs[2 * n].at[i]) for i in range(n)]
    for copy in copies:
        copy.start()
    for copy in copies:
        copy.wait()


def local(consts, fine_in, mid_in, coarse_in, lateral_weight, out_weight, cotangent):
    def flat(v):
        return v.reshape(-1, v.shape[-1])

    args = [flat(fine_in), flat(mid_in), flat(coarse_in), lateral_weight, out_weight, flat(cotangent)]
    args += [jnp.asarray(v) for v in consts.values()]
    hbm = pl.BlockSpec(memory_space=pl.ANY)
    vmem = pl.BlockSpec(memory_space=pltpu.VMEM)
    outs = pl.pallas_call(
        functools.partial(kernel, tuple(consts)),
        out_shape=[
            jax.ShapeDtypeStruct((512, C), BF),
            jax.ShapeDtypeStruct((512, C), BF),
            jax.ShapeDtypeStruct((128, C), BF),
            jax.ShapeDtypeStruct((32, C), BF),
            jax.ShapeDtypeStruct((12, 32), F32),
            jax.ShapeDtypeStruct((32, 36), F32),
        ],
        in_specs=[hbm] * len(args),
        out_specs=[hbm] * 4 + [vmem] * 2,
        scratch_shapes=list(SCRATCH.values()),
        compiler_params=pltpu.CompilerParams(
            collective_id=0, has_side_effects=True, vmem_limit_bytes=63 * 2**20
        ),
        cost_estimate=pl.CostEstimate(flops=2_400_000_000, bytes_accessed=4_000_000, transcendentals=262144),
    )(*args)
    outs = pl.pallas_call(
        hand_on,
        out_shape=[jax.ShapeDtypeStruct(v.shape, v.dtype) for v in outs],
        in_specs=[hbm] * len(outs),
        out_specs=[hbm] * len(outs),
        scratch_shapes=[pltpu.SemaphoreType.DMA((len(outs),))],
        compiler_params=pltpu.CompilerParams(vmem_limit_bytes=63 * 2**20),
    )(*outs)
    return (
        outs[0].reshape(fine_in.shape),
        outs[1].reshape(fine_in.shape),
        outs[2].reshape(mid_in.shape),
        outs[3].reshape(coarse_in.shape),
        outs[4],
        outs[5].T,
    )


def solution(mesh):
    field = P("rows", "cols", None)
    return jax.shard_map(
        functools.partial(local, constants()),
        mesh=mesh,
        in_specs=(field, field, field, P(), P(), field),
        out_specs=(field, field, field, field, P("cols", "rows"), P("cols", "rows")),
        check_vma=False,
    )
```

```python
import functools
from types import SimpleNamespace

import jax
import jax.numpy as jnp
import ml_dtypes
import numpy as np
from jax import lax
from jax.experimental import pallas as pl
from jax.experimental.pallas import tpu as pltpu
from jax.sharding import PartitionSpec as P

BF = jnp.bfloat16
F32 = jnp.float32
MESH = pl.DeviceIdType.MESH
C = 256
NR, NC = 8, 64
LANE = 128


def place(h, w, i, j):
    if j < 0:
        return w * (h + 2) + i + 1
    if j >= w:
        return w * (h + 2) + 16 + i + 1
    return (i + 1) * w + j


def size(h, w):
    return w * (h + 2) + 32


def cells(h, w):
    return [(i, j) for i in range(-1, h + 1) for j in range(-1, w + 1)]


def clamp(i, n, kind):
    if kind == 1:
        i = max(i, 0)
    if kind == 2:
        i = min(i, n - 1)
    return i


def up_taps(i):
    k = i // 2
    if i % 2 == 0:
        return [(k - 1, 0.25), (k, 0.75)]
    return [(k, 0.75), (k + 1, 0.25)]


def up_matrix(h, w, pad):
    mat = np.zeros((9, size(2 * h, 2 * w), pad), np.float32)
    for v in range(9):
        for i, j in cells(2 * h, 2 * w):
            for ri, rw in up_taps(i):
                for ci, cw in up_taps(j):
                    ri2, ci2 = clamp(ri, h, v // 3), clamp(ci, w, v % 3)
                    mat[v, place(2 * h, 2 * w, i, j), place(h, w, ri2, ci2)] += rw * cw
    return mat.astype(ml_dtypes.bfloat16)


def down_matrix(h, w, rows, pad):
    mat = np.zeros((9, rows, pad), np.float32)
    weights = (0.25, 0.75, 0.75, 0.25)
    for v in range(9):
        for i in range(h):
            for j in range(w):
                for a in range(4):
                    for b in range(4):
                        ri = clamp(2 * i - 1 + a, 2 * h, v // 3)
                        ci = clamp(2 * j - 1 + b, 2 * w, v % 3)
                        mat[v, i * w + j, place(2 * h, 2 * w, ri, ci)] += weights[a] * weights[b]
    return mat.astype(ml_dtypes.bfloat16)


def down_line(n, kind):
    line = np.zeros((n + 2, 2 * n + 4))
    for k in range(-1, n + 1):
        if (kind == 1 and k < 0) or (kind == 2 and k >= n):
            continue
        for a, weight in enumerate((0.25, 0.75, 0.75, 0.25)):
            f = clamp(2 * k - 1 + a, 2 * n, kind)
            if -2 <= f < 2 * n + 2:
                line[k + 1, f + 2] += weight
    return line


def adjoint_matrix(h, w, steps, pad):
    fh, fw = h << steps, w << steps
    mat = np.zeros((9, fh * fw, pad), np.float32)
    for v in range(9):
        lines = []
        for n, kind in ((h, v // 3), (w, v % 3)):
            line = down_line(n, kind)
            for s in range(1, steps):
                line = line[:, 1:-1] @ down_line(n << s, kind)
            lines.append(line[:, 2:-2])
        both = np.multiply.outer(*lines)
        for i in range(-1, h + 1):
            for j in range(-1, w + 1):
                mat[v, :, place(h, w, i, j)] = both[i + 1, :, j + 1, :].reshape(-1)
    return mat.astype(ml_dtypes.bfloat16)


def pack_matrix(h, w, first, cols):
    mat = np.zeros((32, cols), np.float32)
    for i in range(h):
        mat[first + i, i * w] = 1
        mat[16 + first + i, i * w + w - 1] = 1
    return mat.astype(ml_dtypes.bfloat16)


def side_matrix(levels):
    mat = np.zeros((32 * len(levels), LANE), np.float32)
    for n, (h, first) in enumerate(levels):
        for side in range(2):
            row, src = 32 * n + 16 * side, 48 * side
            mat[row, src + 16 + first + h - 1] = 1
            for i in range(h):
                mat[row + 1 + i, src + first + i] = 1
            mat[row + 1 + h, src + 32 + first] = 1
    return mat.astype(ml_dtypes.bfloat16)


def constants():
    packs = [
        pack_matrix(8, 64, 0, 512),
        pack_matrix(4, 32, 8, 128),
        pack_matrix(2, 16, 12, 32),
        pack_matrix(4, 32, 0, 128),
    ]
    return dict(
        u1=up_matrix(2, 16, 128),
        u2=up_matrix(4, 32, 256),
        d1=down_matrix(4, 32, 128, 768),
        d2=down_matrix(2, 16, 128, 256),
        a1=adjoint_matrix(4, 32, 1, 256),
        a2=adjoint_matrix(2, 16, 2, 128),
        pf=packs[0],
        pm=packs[1],
        pc=np.concatenate([packs[2], np.zeros((32, 96), ml_dtypes.bfloat16)], 1),
        pm0=packs[3],
        s1=side_matrix([(8, 0), (4, 8), (2, 12)]),
        sf=side_matrix([(8, 0)]),
        sm=side_matrix([(4, 0)]),
    )


CP, CQ, LP, LQ = 640, 512, 128, 256


def dot(a, b):
    return jnp.dot(a, b, preferred_element_type=F32)


def dot_t(a, b):
    return lax.dot_general(a, b, (((1,), (1,)), ((), ())), preferred_element_type=F32)


def kernel(consts, *refs):
    fin, mid, coa, wl, wo_hbm, cot = refs[:6]
    k = SimpleNamespace(**dict(zip(consts, refs[6 : 6 + len(consts)])))
    o_mask, o_fine, o_mid, o_coa, o_lat, o_conv = refs[6 + len(consts) : 12 + len(consts)]
    g = SimpleNamespace(**dict(zip(SCRATCH, refs[12 + len(consts) :])))
    r, c = lax.axis_index("rows"), lax.axis_index("cols")
    y, x_lo = r // 2, r % 2
    x_hi, z, core = c // 32, (c // 2) % 16, c % 2
    x = x_hi * 2 + x_lo
    other = 1 - core
    e_n, e_s = 1 - (r + NR - 1) // NR, (r + 1) // NR
    e_w, e_e = 1 - (c + NC - 1) // NC, (c + 1) // NC
    variant = (e_n + 2 * e_s) * 3 + e_w + 2 * e_e

    up, down = (r + NR - 1) % NR, (r + 1) % NR
    left, right = (c + NC - 1) % NC, (c + 1) % NC

    def dev_x(d):
        t = (x + d) % 4
        return (y * 2 + t % 2, (t // 2) * 32 + z * 2 + core), t

    def dev_y(d):
        t = (y + d) % 4
        return (t * 2 + x_lo, c), t

    def dev_z(d):
        t = (z + d) % 16
        return (r, x_hi * 32 + t * 2 + core), t

    partner = (r, x_hi * 32 + z * 2 + other)

    loads = []

    def load(src, dst):
        copy = pltpu.make_async_copy(src, dst, g.lsem.at[len(loads)])
        copy.start()
        loads.append(copy)
        return copy

    inputs = [
        load(fin, g.finx.at[64:576]),
        load(mid, g.midx.at[32:160]),
        load(coa, g.coax.at[16:48]),
        load(coa, g.coab.at[0:32]),
        load(k.pf, g.v_pf),
        load(k.pm, g.v_pm),
        load(k.pc, g.v_pc),
    ]
    forward = [
        load(k.s1, g.v_s1),
        load(wl, g.v_wl),
        load(k.u1.at[variant], g.v_u1),
        load(k.u2.at[variant], g.v_u2),
        load(k.a1.at[variant], g.v_a1),
        load(k.a2.at[variant], g.v_a2),
    ]
    load_wo = load(wo_hbm, g.v_wo)
    load_cot = load(cot, g.v_cot)
    load_sf = load(k.sf, g.v_sf)
    backward = [
        load(k.d1.at[variant], g.v_d1),
        load(k.d2.at[variant], g.v_d2),
        load(k.pm0, g.v_pm0),
        load(k.sm, g.v_sm),
    ]

    def wait(copies):
        for copy in copies:
            copy.wait()

    peers = [(up, c), (down, c)] + [(a, b) for a in (r, up, down) for b in (left, right)]
    for d in (1, 2, 3):
        peers += [dev_x(d)[0], dev_y(d)[0]]
    peers += [dev_z(1)[0], dev_z(15)[0]]
    barrier = pltpu.get_barrier_semaphore()
    for p in peers:
        pl.semaphore_signal(barrier, inc=1, device_id=p, device_id_type=MESH)

    def greet(n):
        for d in (1 << n, 16 - (1 << n)):
            pl.semaphore_signal(g.far.at[n], inc=1, device_id=dev_z(d)[0], device_id_type=MESH)

    def met(n):
        pl.semaphore_wait(g.far.at[n], 2)

    for ref, at, count in ((g.coab, 32, 96), (g.midx, 224, 32), (g.coax, 96, 32), (g.topb, 96, 32), (g.midb, 224, 32), (g.dfx, 672, 96), (g.dmx, 224, 32)):
        ref[at : at + count] = jnp.zeros((count, C), BF)
    for ref in (g.rs1, g.rs2, g.rs3, g.rs4):
        ref[96:128] = jnp.zeros((32, C), BF)

    used = [0]

    def send(src, dst, to):
        n = used[0]
        used[0] += 1
        copy = pltpu.make_async_remote_copy(
            src_ref=src,
            dst_ref=dst,
            send_sem=g.ssem.at[n],
            recv_sem=g.rsem.at[n],
            device_id=to,
            device_id_type=MESH,
        )
        copy.start()
        return copy

    sent = []

    def received(copies):
        for copy in copies:
            copy.wait_recv()
        sent.extend(copies)

    def send_rows(buf, h, w):
        return [
            send(buf.at[w : 2 * w], buf.at[w * (h + 1) : w * (h + 2)], (up, c)),
            send(buf.at[w * h : w * (h + 1)], buf.at[0:w], (down, c)),
        ]

    def send_sides(pack, slots):
        west, east = pack.at[0:16], pack.at[16:32]

        def slot(n):
            return slots.at[16 * n : 16 * n + 16]

        return [
            send(east, slot(0), (r, right)),
            send(east, slot(1), (down, right)),
            send(east, slot(2), (up, right)),
            send(west, slot(3), (r, left)),
            send(west, slot(4), (down, left)),
            send(west, slot(5), (up, left)),
        ]

    wait(inputs)
    packed = dot(g.v_pf[...], g.finx[64:576])
    packed += dot(g.v_pm[...], g.midx[32:160])
    packed += dot(g.v_pc[...], g.coab[...])
    g.pk1[...] = packed.astype(BF)
    pl.semaphore_wait(barrier, len(peers))
    halo = send_sides(g.pk1, g.rs1)
    halo += send_rows(g.coax, 2, 16)
    halo += send_rows(g.midx, 4, 32)
    halo += send_rows(g.finx, 8, 64)
    greet(0)
    wait(forward)
    wl = g.v_wl
    w_fine, w_mid, w_top = wl[0:C], wl[C : 2 * C], wl[2 * C : 3 * C]
    fex = g.fex
    fex[64:576] = dot(g.finx[64:576], w_fine)
    received(halo)
    met(0)
    greet(1)
    sides = dot(g.v_s1[...], g.rs1[...]).astype(BF)
    g.finx[640:672] = sides[0:32]
    g.midx[192:224] = sides[32:64]
    g.coax[64:96] = sides[64:96]

    g.topb[0:96] = dot(g.coax[0:96], w_top).astype(BF)
    g.midb[0:224] = (dot(g.midx[0:224], w_mid) + dot(g.v_u1[...], g.topb[...])).astype(BF)
    fex[0:64] = dot(g.finx[0:64], w_fine)
    fex[576:672] = dot(g.finx[576:672], w_fine)
    fex[...] += dot(g.v_u2[...], g.midb[...])

    keep_n, keep_s = (1 - e_n).astype(F32), (1 - e_s).astype(F32)
    keep_w, keep_e = (1 - e_w).astype(F32), (1 - e_e).astype(F32)
    line = lax.broadcasted_iota(jnp.int32, (16, C), 0)
    keep_rows = jnp.where(line == 0, keep_n, jnp.where(line == 9, keep_s, 1.0))

    def spread(north, body, south, west, east, out, flip):
        s = g.shift
        s[0, 8:72] = north * keep_n
        s[1:9, 8:72] = body.reshape(8, 64, C)
        s[9, 8:72] = south * keep_s
        west = west * (keep_rows * keep_w)
        east = east * (keep_rows * keep_e)
        for i in range(10):
            s[i, 7:8] = west[i : i + 1]
            s[i, 72:73] = east[i : i + 1]
        for b in range(3):
            at = 9 - b if flip else 7 + b
            out[:, b * C : (b + 1) * C] = s[:, at : at + 64].astype(BF).reshape(640, C)

    spread(fex[0:64], fex[64:576], fex[576:640], fex[640:656], fex[656:672], g.fsh, False)

    load_wo.wait()
    wo, fsh, dsh = g.v_wo, g.fsh, g.dsh
    g.pre[...] = sum(dot(fsh[64 * a : 64 * a + 512], wo[768 * a : 768 * a + 768]) for a in range(3))
    load_cot.wait()

    def activate(q, carry):
        at = pl.multiple_of(q * 64, 64)
        v = g.pre[pl.ds(at, 64)]
        half = 0.5 + 0.5 * lax.erf(v * np.float32(np.sqrt(0.5)))
        g.maskb[pl.ds(at, 64)] = (v * half).astype(BF)
        slope = half + v * (jnp.exp(-0.5 * v * v) * np.float32(1 / np.sqrt(2 * np.pi)))
        g.dpx[pl.ds(at + 64, 64)] = (g.v_cot[pl.ds(at, 64)].astype(F32) * slope).astype(BF)
        return carry

    lax.fori_loop(0, 8, activate, 0)
    g.xm[...] = dot(g.v_a1[...], g.midx[...]).astype(BF)
    g.xc[...] = dot(g.v_a2[...], g.coax[...]).astype(BF)
    stores = []

    def store(src, dst):
        copy = pltpu.make_async_copy(src, dst, g.osem.at[len(stores)])
        copy.start()
        stores.append(copy)

    store(g.maskb, o_mask)

    load_sf.wait()
    halo = send_rows(g.dpx, 8, 64)
    g.pk2[...] = dot(g.v_pf[...], g.dpx[64:576]).astype(BF)
    halo += send_sides(g.pk2, g.rs2)

    grad, got = g.grad, g.got
    dpre_t = g.dpx[64:576].T
    pair = []
    for a in range(3):
        lanes = pl.ds(768 * a, 768)
        term = dot(dpre_t, fsh[64 * a : 64 * a + 512]).astype(BF)
        grad[:, :, :, lanes] = term.reshape(8, 2, 16, 768)
        pair.append(send(grad.at[:, other, :, lanes], got.at[:, :, lanes], partner))

    def begin(buf, slots, dev):
        out = []
        for d in (1, 2, 3):
            to, t = dev(d)
            out.append(send(buf.at[t], slots.at[d - 1], to))
        return out

    def total(buf, mine, slots):
        return buf[mine].astype(F32) + slots[0].astype(F32) + slots[1].astype(F32) + slots[2].astype(F32)

    def split(mine, theirs, half, first, p, q):
        wp, wq = p.shape[-1], q.shape[-1]
        for n in range(8):
            part = (mine[n, core].astype(F32) + theirs[n].astype(F32)).astype(BF)
            for h in range(2):
                at = half * h
                p[2 * h + n % 2, n // 2] = part[:, at : at + wp]
                q[n // 2, 2 * h + n % 2] = part[:, at + wp : at + wp + wq]

    received(pair)
    split(grad, got, 1152, 0, g.cp1, g.cq1)
    cp = begin(g.cp1, g.cp1r, dev_x)
    cq = begin(g.cq1, g.cq1r, dev_y)
    met(1)
    greet(2)

    received(halo)
    sides = dot(g.v_sf[...], g.rs2[...])
    dpx = g.dpx
    spread(
        dpx[0:64].astype(F32), dpx[64:576].astype(F32), dpx[576:640].astype(F32),
        sides[0:16], sides[16:32], dsh, True,
    )
    dfine = None
    for a in range(3):
        for b in range(3):
            t = 3 * a + b
            term = dot_t(dsh[64 * (2 - a) : 64 * (2 - a) + 512, b * C : (b + 1) * C], wo[t * C : (t + 1) * C])
            dfine = term if dfine is None else dfine + term
    dfx = g.dfx
    dfx[64:576] = dfine.astype(BF)

    lgrad, lgot = g.lgrad, g.lgot
    dfine_t = dfx[64:576].T
    lpair = []
    for n, rows in enumerate((g.finx[64:576], g.xm[...], g.xc[...])):
        lanes = pl.ds(n * C, C)
        lgrad[:, :, :, lanes] = dot(dfine_t, rows).astype(BF).reshape(8, 2, 16, C)
        lpair.append(send(lgrad.at[:, other, :, lanes], lgot.at[:, :, lanes], partner))
    halo = send_rows(dfx, 8, 64)
    g.pk3[...] = dot(g.v_pf[...], dfx[64:576]).astype(BF)
    halo += send_sides(g.pk3, g.rs3)

    received(lpair)
    split(lgrad, lgot, 384, 0, g.lp1, g.lq1)
    lp = begin(g.lp1, g.lp1r, dev_x)
    lq = begin(g.lq1, g.lq1r, dev_y)

    received(cp)
    g.cp2[...] = total(g.cp1, x, g.cp1r).astype(BF)
    cp = begin(g.cp2, g.cp2r, dev_y)
    received(cq)
    g.cq2[...] = total(g.cq1, y, g.cq1r).astype(BF)
    cq = begin(g.cq2, g.cq2r, dev_x)

    received(lp)
    g.lp2[...] = total(g.lp1, x, g.lp1r).astype(BF)
    lp = begin(g.lp2, g.lp2r, dev_y)
    received(lq)
    g.lq2[...] = total(g.lq1, y, g.lq1r).astype(BF)
    lq = begin(g.lq2, g.lq2r, dev_x)

    received(halo)
    wait(backward)
    dfx[640:672] = dot(g.v_sf[...], g.rs3[...]).astype(BF)
    dmx = g.dmx
    dmx[32:160] = dot(g.v_d1[...], dfx[...]).astype(BF)
    halo = send_rows(dmx, 4, 32)
    g.pk4[...] = dot(g.v_pm0[...], dmx[32:160]).astype(BF)
    halo += send_sides(g.pk4, g.rs4)

    sums = g.sums
    received(cp)
    sums[:, 0:CP] = total(g.cp2, y, g.cp2r)
    received(cq)
    sums[:, CP : CP + CQ] = total(g.cq2, x, g.cq2r)
    received(lp)
    sums[:, 1152 : 1152 + LP] = total(g.lp2, y, g.lp2r)
    received(lq)
    sums[:, 1152 + LP : 1536] = total(g.lq2, x, g.lq2r)

    lane = lax.broadcasted_iota(jnp.int32, (16, LANE), 1)

    def window(base, count, start):
        t, off = start // LANE, start % LANE

        def tile(n):
            n = min(max(n, 0), count // LANE - 1)
            return sums[:, base + n * LANE : base + (n + 1) * LANE]

        if off == 0:
            return tile(t)
        return jnp.where(
            lane < LANE - off,
            pltpu.roll(tile(t), LANE - off, 1),
            pltpu.roll(tile(t + 1), LANE - off, 1),
        )

    for n in range(16):
        conv = window(0, 1152, 72 * n)
        lat = window(1152, 384, 24 * n - 72)
        g.z1[n] = jnp.where(lane < 72, conv, lat).astype(BF)
    met(2)
    zc = []
    for d in range(1, 16):
        to, t = dev_z(d)
        zc.append(send(g.z1.at[t], g.z1r.at[d - 1], to))

    g.fgb[...] = dot_t(dfx[64:576], w_fine).astype(BF)
    store(g.fgb, o_fine)
    g.mgb[...] = dot_t(dmx[32:160], w_mid).astype(BF)
    store(g.mgb, o_mid)
    received(halo)
    dmx[192:224] = dot(g.v_sm[...], g.rs4[...]).astype(BF)
    dtop = dot(g.v_d2[...], dmx[...]).astype(BF)
    g.cgb[...] = dot_t(dtop[0:32], w_top).astype(BF)
    store(g.cgb, o_coa)

    received(zc)
    same = g.z1[z].astype(F32)
    for d in range(15):
        same += g.z1r[d].astype(F32)
    g.z2[...] = same.astype(BF)
    received([send(g.z2, g.z2r, partner)])
    cross = g.z2r[...].astype(F32)
    first = core == 0
    both = jnp.concatenate([jnp.where(first, same, cross), jnp.where(first, cross, same)], 0)
    o_conv[...] = jnp.where(first, both[:, 0:36], pltpu.roll(both, LANE - 36, 1)[:, 0:36])
    g.turn[...] = jnp.concatenate([both, jnp.zeros((96, LANE), F32)], 0).T
    o_lat[...] = jnp.where(first, g.turn[72:84, 0:32], g.turn[84:96, 0:32])

    for copy in sent:
        copy.wait_send()
    wait(stores)


VM = pltpu.VMEM
DMA = pltpu.SemaphoreType.DMA
SCRATCH = dict(
    finx=VM((672, C), BF),
    midx=VM((256, C), BF),
    coax=VM((128, C), BF),
    coab=VM((128, C), BF),
    v_wl=VM((768, C), BF),
    v_wo=VM((2304, C), BF),
    v_cot=VM((512, C), BF),
    v_u1=VM((224, 128), BF),
    v_u2=VM((672, 256), BF),
    v_d1=VM((128, 768), BF),
    v_d2=VM((128, 256), BF),
    v_pf=VM((32, 512), BF),
    v_pm=VM((32, 128), BF),
    v_pc=VM((32, 128), BF),
    v_pm0=VM((32, 128), BF),
    v_s1=VM((96, 128), BF),
    v_sf=VM((32, 128), BF),
    v_sm=VM((32, 128), BF),
    topb=VM((128, C), BF),
    midb=VM((256, C), BF),
    fex=VM((672, C), F32),
    shift=VM((10, 80, C), F32),
    fsh=VM((640, 768), BF),
    dsh=VM((640, 768), BF),
    pre=VM((512, C), F32),
    maskb=VM((512, C), BF),
    dpx=VM((640, C), BF),
    dfx=VM((768, C), BF),
    dmx=VM((256, C), BF),
    fgb=VM((512, C), BF),
    mgb=VM((128, C), BF),
    cgb=VM((32, C), BF),
    pk1=VM((32, C), BF),
    pk2=VM((32, C), BF),
    pk3=VM((32, C), BF),
    pk4=VM((32, C), BF),
    rs1=VM((128, C), BF),
    rs2=VM((128, C), BF),
    rs3=VM((128, C), BF),
    rs4=VM((128, C), BF),
    grad=VM((8, 2, 16, 2304), BF),
    got=VM((8, 16, 2304), BF),
    lgrad=VM((8, 2, 16, 768), BF),
    lgot=VM((8, 16, 768), BF),
    cp1=VM((4, 4, 16, CP), BF),
    cp1r=VM((3, 4, 16, CP), BF),
    cp2=VM((4, 16, CP), BF),
    cp2r=VM((3, 16, CP), BF),
    cq1=VM((4, 4, 16, CQ), BF),
    cq1r=VM((3, 4, 16, CQ), BF),
    cq2=VM((4, 16, CQ), BF),
    cq2r=VM((3, 16, CQ), BF),
    lp1=VM((4, 4, 16, LP), BF),
    lp1r=VM((3, 4, 16, LP), BF),
    lp2=VM((4, 16, LP), BF),
    lp2r=VM((3, 16, LP), BF),
    lq1=VM((4, 4, 16, LQ), BF),
    lq1r=VM((3, 4, 16, LQ), BF),
    lq2=VM((4, 16, LQ), BF),
    lq2r=VM((3, 16, LQ), BF),
    sums=VM((16, 1536), F32),
    z1=VM((16, 16, LANE), BF),
    z1r=VM((15, 16, LANE), BF),
    z2=VM((16, LANE), BF),
    z2r=VM((16, LANE), BF),
    far=pltpu.SemaphoreType.REGULAR((3,)),
    v_a1=VM((512, 256), BF),
    v_a2=VM((512, 128), BF),
    xm=VM((512, C), BF),
    xc=VM((512, C), BF),
    turn=VM((128, 128), F32),
    lsem=DMA((24,)),
    osem=DMA((4,)),
    ssem=DMA((96,)),
    rsem=DMA((96,)),
)


def hand_on(*refs):
    n = len(refs) // 3
    ins, outs, held, sems = refs[:n], refs[n : 2 * n], refs[2 * n : 3 * n], refs[3 * n]
    arrive = [pltpu.make_async_copy(ins[i], held[i], sems.at[0, i]) for i in range(n)]
    leave = [pltpu.make_async_copy(held[i], outs[i], sems.at[1, i]) for i in range(n)]
    for copy in arrive:
        copy.start()
    for i in reversed(range(n)):
        arrive[i].wait()
        leave[i].start()
    for copy in leave:
        copy.wait()


def local(consts, fine_in, mid_in, coarse_in, lateral_weight, out_weight, cotangent):
    def flat(v):
        return v.reshape(-1, v.shape[-1])

    args = [flat(fine_in), flat(mid_in), flat(coarse_in), lateral_weight, out_weight, flat(cotangent)]
    args += [jnp.asarray(v) for v in consts.values()]
    hbm = pl.BlockSpec(memory_space=pl.ANY)
    vmem = pl.BlockSpec(memory_space=pltpu.VMEM)
    outs = pl.pallas_call(
        functools.partial(kernel, tuple(consts)),
        out_shape=[
            jax.ShapeDtypeStruct((512, C), BF),
            jax.ShapeDtypeStruct((512, C), BF),
            jax.ShapeDtypeStruct((128, C), BF),
            jax.ShapeDtypeStruct((32, C), BF),
            jax.ShapeDtypeStruct((12, 32), F32),
            jax.ShapeDtypeStruct((32, 36), F32),
        ],
        in_specs=[hbm] * len(args),
        out_specs=[hbm] * 4 + [vmem] * 2,
        scratch_shapes=list(SCRATCH.values()),
        compiler_params=pltpu.CompilerParams(
            collective_id=0, has_side_effects=True, vmem_limit_bytes=63 * 2**20
        ),
        cost_estimate=pl.CostEstimate(flops=2_400_000_000, bytes_accessed=4_000_000, transcendentals=262144),
    )(*args)
    outs = pl.pallas_call(
        hand_on,
        out_shape=[jax.ShapeDtypeStruct(v.shape, v.dtype) for v in outs],
        in_specs=[hbm] * len(outs),
        out_specs=[hbm] * len(outs),
        scratch_shapes=[VM(v.shape, v.dtype) for v in outs] + [DMA((2, len(outs)))],
        compiler_params=pltpu.CompilerParams(vmem_limit_bytes=63 * 2**20),
    )(*outs)
    return (
        outs[0].reshape(fine_in.shape),
        outs[1].reshape(fine_in.shape),
        outs[2].reshape(mid_in.shape),
        outs[3].reshape(coarse_in.shape),
        outs[4],
        outs[5].T,
    )


def solution(mesh):
    field = P("rows", "cols", None)
    return jax.shard_map(
        functools.partial(local, constants()),
        mesh=mesh,
        in_specs=(field, field, field, P(), P(), field),
        out_specs=(field, field, field, field, P("cols", "rows"), P("cols", "rows")),
        check_vma=False,
    )
```

```python
import functools
from types import SimpleNamespace

import jax
import jax.numpy as jnp
import ml_dtypes
import numpy as np
from jax import lax
from jax.experimental import pallas as pl
from jax.experimental.pallas import tpu as pltpu
from jax.sharding import PartitionSpec as P

BF = jnp.bfloat16
F32 = jnp.float32
MESH = pl.DeviceIdType.MESH
C = 256
NR, NC = 8, 64
LANE = 128


def place(h, w, i, j):
    if j < 0:
        return w * (h + 2) + i + 1
    if j >= w:
        return w * (h + 2) + 16 + i + 1
    return (i + 1) * w + j


def size(h, w):
    return w * (h + 2) + 32


def cells(h, w):
    return [(i, j) for i in range(-1, h + 1) for j in range(-1, w + 1)]


def clamp(i, n, kind):
    if kind == 1:
        i = max(i, 0)
    if kind == 2:
        i = min(i, n - 1)
    return i


def up_taps(i):
    k = i // 2
    if i % 2 == 0:
        return [(k - 1, 0.25), (k, 0.75)]
    return [(k, 0.75), (k + 1, 0.25)]


def up_matrix(h, w, pad):
    mat = np.zeros((9, size(2 * h, 2 * w), pad), np.float32)
    for v in range(9):
        for i, j in cells(2 * h, 2 * w):
            for ri, rw in up_taps(i):
                for ci, cw in up_taps(j):
                    ri2, ci2 = clamp(ri, h, v // 3), clamp(ci, w, v % 3)
                    mat[v, place(2 * h, 2 * w, i, j), place(h, w, ri2, ci2)] += rw * cw
    return mat.astype(ml_dtypes.bfloat16)


def down_line(n, kind):
    line = np.zeros((n + 2, 2 * n + 4))
    for k in range(-1, n + 1):
        if (kind == 1 and k < 0) or (kind == 2 and k >= n):
            continue
        for a, weight in enumerate((0.25, 0.75, 0.75, 0.25)):
            f = clamp(2 * k - 1 + a, 2 * n, kind)
            if -2 <= f < 2 * n + 2:
                line[k + 1, f + 2] += weight
    return line


def adjoint_matrix(h, w, steps, rows, pad):
    fh, fw = h << steps, w << steps
    mat = np.zeros((9, rows, pad), np.float32)
    for v in range(9):
        lines = []
        for n, kind in ((h, v // 3), (w, v % 3)):
            line = down_line(n, kind)
            for s in range(1, steps):
                line = line[:, 1:-1] @ down_line(n << s, kind)
            lines.append(line[:, 1:-1])
        both = np.multiply.outer(*lines)
        spots = [place(fh, fw, a, b) for a, b in cells(fh, fw)]
        for i, j in cells(h, w):
            mat[v, spots, place(h, w, i, j)] = both[i + 1, :, j + 1, :].reshape(-1)
    return mat.astype(ml_dtypes.bfloat16)


def rim_matrix():
    mat = np.zeros((96, 512), np.float32)
    for a in range(3):
        for q in range(10):
            i = q - a
            if 0 <= i < 8:
                mat[16 * a + q, i * 64] = 1
                mat[48 + 16 * a + q, i * 64 + 63] = 1
    return mat.astype(ml_dtypes.bfloat16)


def scatter_matrix(h, w, level):
    mat = np.zeros((h * w, 384), np.float32)
    for side, j in ((0, 0), (1, w - 1)):
        at = 144 * side + 16 * level
        for i in range(h):
            mat[i * w + j, at + 1 + i] += 1
        mat[j, at + 48 + h + 1] += 1
        mat[(h - 1) * w + j, at + 96] += 1
    return mat.astype(ml_dtypes.bfloat16)


def pack_matrix(h, w, first, cols):
    mat = np.zeros((32, cols), np.float32)
    for i in range(h):
        mat[first + i, i * w] = 1
        mat[16 + first + i, i * w + w - 1] = 1
    return mat.astype(ml_dtypes.bfloat16)


def side_matrix(levels):
    mat = np.zeros((32 * len(levels), LANE), np.float32)
    for n, (h, first) in enumerate(levels):
        for side in range(2):
            row, src = 32 * n + 16 * side, 48 * side
            mat[row, src + 16 + first + h - 1] = 1
            for i in range(h):
                mat[row + 1 + i, src + first + i] = 1
            mat[row + 1 + h, src + 32 + first] = 1
    return mat.astype(ml_dtypes.bfloat16)


def constants():
    packs = [
        pack_matrix(8, 64, 0, 512),
        pack_matrix(4, 32, 8, 128),
        pack_matrix(2, 16, 12, 32),
    ]
    a1 = adjoint_matrix(4, 32, 1, 768, 256)
    return dict(
        u1=up_matrix(2, 16, 128),
        u2=up_matrix(4, 32, 256),
        a1=a1,
        a2=adjoint_matrix(2, 16, 2, 768, 128),
        d1=np.ascontiguousarray(a1.transpose(0, 2, 1)[:, :224]),
        d2=np.ascontiguousarray(adjoint_matrix(2, 16, 1, 256, 96).transpose(0, 2, 1)),
        pf=packs[0],
        pm=packs[1],
        pc=np.concatenate([packs[2], np.zeros((32, 96), ml_dtypes.bfloat16)], 1),
        s1=side_matrix([(8, 0), (4, 8), (2, 12)]),
        rim=rim_matrix(),
        tf=scatter_matrix(8, 64, 0),
        tm=scatter_matrix(4, 32, 1),
        tc=scatter_matrix(2, 16, 2),
    )


CP, CQ, LP, LQ = 640, 512, 128, 256


def dot(a, b):
    return jnp.dot(a, b, preferred_element_type=F32)


def dot_t(a, b):
    return lax.dot_general(a, b, (((1,), (1,)), ((), ())), preferred_element_type=F32)


def kernel(consts, *refs):
    fin, mid, coa, wl, wo_hbm, cot = refs[:6]
    k = SimpleNamespace(**dict(zip(consts, refs[6 : 6 + len(consts)])))
    o_mask, o_fine, o_mid, o_coa, o_lat, o_conv = refs[6 + len(consts) : 12 + len(consts)]
    g = SimpleNamespace(**dict(zip(SCRATCH, refs[12 + len(consts) :])))
    r, c = lax.axis_index("rows"), lax.axis_index("cols")
    y, x_lo = r // 2, r % 2
    x_hi, z, core = c // 32, (c // 2) % 16, c % 2
    x = x_hi * 2 + x_lo
    other = 1 - core
    e_n, e_s = 1 - (r + NR - 1) // NR, (r + 1) // NR
    e_w, e_e = 1 - (c + NC - 1) // NC, (c + 1) // NC
    variant = (e_n + 2 * e_s) * 3 + e_w + 2 * e_e

    up, down = (r + NR - 1) % NR, (r + 1) % NR
    left, right = (c + NC - 1) % NC, (c + 1) % NC

    def dev_x(d):
        t = (x + d) % 4
        return (y * 2 + t % 2, (t // 2) * 32 + z * 2 + core), t

    def dev_y(d):
        t = (y + d) % 4
        return (t * 2 + x_lo, c), t

    def dev_z(d):
        t = (z + d) % 16
        return (r, x_hi * 32 + t * 2 + core), t

    partner = (r, x_hi * 32 + z * 2 + other)

    peers = [(up, c), (down, c)] + [(a, b) for a in (r, up, down) for b in (left, right)]
    for d in (1, 2, 3):
        peers += [dev_x(d)[0], dev_y(d)[0]]
    peers += [dev_z(1)[0], dev_z(15)[0]]
    barrier = pltpu.get_barrier_semaphore()
    for p in peers:
        pl.semaphore_signal(barrier, inc=1, device_id=p, device_id_type=MESH)

    def greet(n):
        for d in (1 << n, 16 - (1 << n)):
            pl.semaphore_signal(g.far.at[n], inc=1, device_id=dev_z(d)[0], device_id_type=MESH)

    def met(n):
        pl.semaphore_wait(g.far.at[n], 2)

    loads = []

    def load(src, dst):
        copy = pltpu.make_async_copy(src, dst, g.lsem.at[len(loads)])
        copy.start()
        loads.append(copy)
        return copy

    inputs = [
        load(fin, g.finx.at[64:576]),
        load(mid, g.midx.at[32:160]),
        load(coa, g.coax.at[16:48]),
        load(coa, g.coab.at[0:32]),
        load(k.pf, g.v_pf),
        load(k.pm, g.v_pm),
        load(k.pc, g.v_pc),
    ]
    forward = [
        load(k.s1, g.v_s1),
        load(wl, g.v_wl),
        load(k.u1.at[variant], g.v_u1),
        load(k.u2.at[variant], g.v_u2),
    ]
    def wait(copies):
        for copy in copies:
            copy.wait()

    blank = ((g.coab, 32, 96), (g.midx, 224, 32), (g.coax, 96, 32), (g.topb, 96, 32), (g.midb, 224, 32))
    blank += ((g.finx, 672, 96), (g.dfx, 672, 96), (g.dmx, 224, 32), (g.rs1, 96, 32), (g.rs2, 288, 96))
    for ref, at, count in blank:
        ref[at : at + count] = jnp.zeros((count, C), BF)
    for at in (0, 1, 10, 11):
        g.shift0[at] = jnp.zeros((80, C), F32)
    for at in (0, 72):
        g.shift0[2:10, at : at + 8] = jnp.zeros((8, 8, C), F32)

    used = [0]

    def send(src, dst, to):
        n = used[0]
        used[0] += 1
        copy = pltpu.make_async_remote_copy(
            src_ref=src,
            dst_ref=dst,
            send_sem=g.ssem.at[n],
            recv_sem=g.rsem.at[n],
            device_id=to,
            device_id_type=MESH,
        )
        copy.start()
        return copy

    sent = []

    def received(copies):
        for copy in copies:
            copy.wait_recv()
        sent.extend(copies)

    def send_rows(buf, h, w):
        return [
            send(buf.at[w : 2 * w], buf.at[w * (h + 1) : w * (h + 2)], (up, c)),
            send(buf.at[w * h : w * (h + 1)], buf.at[0:w], (down, c)),
        ]

    def send_sides(west, east, slots):
        count = west.shape[0]

        def slot(n):
            return slots.at[count * n : count * (n + 1)]

        return [
            send(east, slot(0), (r, right)),
            send(east, slot(1), (down, right)),
            send(east, slot(2), (up, right)),
            send(west, slot(3), (r, left)),
            send(west, slot(4), (down, left)),
            send(west, slot(5), (up, left)),
        ]

    wait(inputs)
    packed = dot(g.v_pf[...], g.finx[64:576])
    packed += dot(g.v_pm[...], g.midx[32:160])
    packed += dot(g.v_pc[...], g.coab[...])
    g.pk1[...] = packed.astype(BF)
    pl.semaphore_wait(barrier, len(peers))
    halo = send_sides(g.pk1.at[0:16], g.pk1.at[16:32], g.rs1)
    halo += send_rows(g.coax, 2, 16)
    halo += send_rows(g.midx, 4, 32)
    halo += send_rows(g.finx, 8, 64)
    greet(0)
    load_wo = load(wo_hbm, g.v_wo)
    load_cot = load(cot, g.v_cot)
    adjoint = [load(k.a1.at[variant], g.v_a1), load(k.a2.at[variant], g.v_a2)]
    backward = [load(k.rim, g.v_rim)]
    closing = [
        load(k.d1.at[variant], g.v_d1),
        load(k.d2.at[variant], g.v_d2),
        load(k.tf, g.v_tf),
        load(k.tm, g.v_tm),
        load(k.tc, g.v_tc),
    ]
    wait(forward)
    wl = g.v_wl
    w_fine, w_mid, w_top = wl[0:C], wl[C : 2 * C], wl[2 * C : 3 * C]
    fex = g.fex
    fex[64:576] = dot(g.finx[64:576], w_fine)
    received(halo)
    met(0)
    greet(1)
    sides = dot(g.v_s1[...], g.rs1[...]).astype(BF)
    g.finx[640:672] = sides[0:32]
    g.midx[192:224] = sides[32:64]
    g.coax[64:96] = sides[64:96]

    g.topb[0:96] = dot(g.coax[0:96], w_top).astype(BF)
    g.midb[0:224] = (dot(g.midx[0:224], w_mid) + dot(g.v_u1[...], g.topb[...])).astype(BF)
    fex[0:64] = dot(g.finx[0:64], w_fine)
    fex[576:672] = dot(g.finx[576:672], w_fine)
    fex[...] += dot(g.v_u2[...], g.midb[...])

    keep_n, keep_s = (1 - e_n).astype(F32), (1 - e_s).astype(F32)
    keep_w, keep_e = (1 - e_w).astype(F32), (1 - e_e).astype(F32)
    line = lax.broadcasted_iota(jnp.int32, (16, C), 0)
    keep_rows = jnp.where(line == 0, keep_n, jnp.where(line == 9, keep_s, 1.0))

    def columns(s, at, out):
        for b in range(3):
            out[:, b * C : (b + 1) * C] = s[:, at[b] : at[b] + 64].astype(BF).reshape(out.shape[0], C)

    s = g.shift
    s[0, 8:72] = fex[0:64] * keep_n
    s[1:9, 8:72] = fex[64:576].reshape(8, 64, C)
    s[9, 8:72] = fex[576:640] * keep_s
    west = fex[640:656] * (keep_rows * keep_w)
    east = fex[656:672] * (keep_rows * keep_e)
    for i in range(10):
        s[i, 7:8] = west[i : i + 1]
        s[i, 72:73] = east[i : i + 1]
    columns(s, (7, 8, 9), g.fsh)

    load_wo.wait()
    wo, fsh, dsh = g.v_wo, g.fsh, g.dsh
    g.pre[...] = sum(dot(fsh[64 * a : 64 * a + 512], wo[768 * a : 768 * a + 768]) for a in range(3))
    load_cot.wait()

    def activate(q, carry):
        at = pl.multiple_of(q * 64, 64)
        v = g.pre[pl.ds(at, 64)]
        half = 0.5 + 0.5 * lax.erf(v * np.float32(np.sqrt(0.5)))
        g.maskb[pl.ds(at, 64)] = (v * half).astype(BF)
        slope = half + v * (jnp.exp(-0.5 * v * v) * np.float32(1 / np.sqrt(2 * np.pi)))
        g.dpx[pl.ds(at, 64)] = (g.v_cot[pl.ds(at, 64)].astype(F32) * slope).astype(BF)
        return carry

    lax.fori_loop(0, 8, activate, 0)
    stores = []

    def store(src, dst):
        copy = pltpu.make_async_copy(src, dst, g.osem.at[len(stores)])
        copy.start()
        stores.append(copy)

    store(g.maskb, o_mask)

    grad, got = g.grad, g.got
    dpre_t = g.dpx[...].T
    pair = []
    for a in range(3):
        lanes = pl.ds(768 * a, 768)
        term = dot(dpre_t, fsh[64 * a : 64 * a + 512]).astype(BF)
        grad[:, :, :, lanes] = term.reshape(8, 2, 16, 768)
        pair.append(send(grad.at[:, other, :, lanes], got.at[:, :, lanes], partner))

    def begin(buf, slots, dev):
        out = []
        for d in (1, 2, 3):
            to, t = dev(d)
            out.append(send(buf.at[t], slots.at[d - 1], to))
        return out

    def total(buf, mine, slots):
        return buf[mine].astype(F32) + slots[0].astype(F32) + slots[1].astype(F32) + slots[2].astype(F32)

    def split(mine, theirs, half, p, q):
        wp, wq = p.shape[-1], q.shape[-1]
        for n in range(8):
            part = (mine[n, core].astype(F32) + theirs[n].astype(F32)).astype(BF)
            for h in range(2):
                at = half * h
                p[2 * h + n % 2, n // 2] = part[:, at : at + wp]
                q[n // 2, 2 * h + n % 2] = part[:, at + wp : at + wp + wq]

    s = g.shift0
    s[2:10, 8:72] = g.dpx[...].astype(F32).reshape(8, 64, C)
    columns(s, (9, 8, 7), dsh)
    wait(backward)
    g.rims[...] = dot(g.v_rim[...], g.dpx[...]).astype(BF)
    body = west = east = None
    for a in range(3):
        for b in range(3):
            block = wo[(3 * a + b) * C : (3 * a + b + 1) * C]
            term = dot_t(dsh[64 * (2 - a) : 64 * (2 - a) + 640, b * C : (b + 1) * C], block)
            body = term if body is None else body + term
            if b == 0:
                term = dot_t(g.rims[16 * a : 16 * a + 16], block)
                west = term if west is None else west + term
            if b == 2:
                term = dot_t(g.rims[48 + 16 * a : 64 + 16 * a], block)
                east = term if east is None else east + term
    dfx = g.dfx
    dfx[0:64] = (body[0:64] * keep_n).astype(BF)
    dfx[64:576] = body[64:576].astype(BF)
    dfx[576:640] = (body[576:640] * keep_s).astype(BF)
    dfx[640:656] = (west * (keep_rows * keep_w)).astype(BF)
    dfx[656:672] = (east * (keep_rows * keep_e)).astype(BF)

    received(pair)
    split(grad, got, 1152, g.cp1, g.cq1)
    cp = begin(g.cp1, g.cp1r, dev_x)
    cq = begin(g.cq1, g.cq1r, dev_y)
    met(1)
    greet(2)

    lgrad, lgot = g.lgrad, g.lgot
    wait(adjoint)
    dfine_t = dfx[...].T
    lpair = []
    for n in range(3):
        lanes = pl.ds(n * C, C)
        if n == 0:
            rows = g.finx[...]
        elif n == 1:
            rows = dot(g.v_a1[...], g.midx[...]).astype(BF)
        else:
            rows = dot(g.v_a2[...], g.coax[...]).astype(BF)
        lgrad[:, :, :, lanes] = dot(dfine_t, rows).astype(BF).reshape(8, 2, 16, C)
        lpair.append(send(lgrad.at[:, other, :, lanes], lgot.at[:, :, lanes], partner))

    wait(closing)
    dmx, dtx = g.dmx, g.dtx
    dmx[0:224] = dot(g.v_d1[...], dfx[...]).astype(BF)
    dtx[...] = dot(g.v_d2[...], dmx[...]).astype(BF)
    north, south, west, east = g.rows_n, g.rows_s, g.cols_w, g.cols_e
    for n, (buf, h, w, at) in enumerate(((dfx, 8, 64, 0), (dmx, 4, 32, 64), (dtx, 2, 16, 96))):
        north[at : at + w] = buf[0:w]
        south[at : at + w] = buf[w * (h + 1) : w * (h + 2)]
        west[16 * n : 16 * n + 16] = buf[w * (h + 2) : w * (h + 2) + 16]
        east[16 * n : 16 * n + 16] = buf[w * (h + 2) + 16 : w * (h + 2) + 32]
    halo = send_sides(west, east, g.rs2)
    halo += [send(north, g.from_s, (up, c)), send(south, g.from_n, (down, c))]

    received(lpair)
    split(lgrad, lgot, 384, g.lp1, g.lq1)
    lp = begin(g.lp1, g.lp1r, dev_x)
    lq = begin(g.lq1, g.lq1r, dev_y)

    received(cp)
    g.cp2[...] = total(g.cp1, x, g.cp1r).astype(BF)
    cp = begin(g.cp2, g.cp2r, dev_y)
    received(cq)
    g.cq2[...] = total(g.cq1, y, g.cq1r).astype(BF)
    cq = begin(g.cq2, g.cq2r, dev_x)

    received(lp)
    g.lp2[...] = total(g.lp1, x, g.lp1r).astype(BF)
    lp = begin(g.lp2, g.lp2r, dev_y)
    received(lq)
    g.lq2[...] = total(g.lq1, y, g.lq1r).astype(BF)
    lq = begin(g.lq2, g.lq2r, dev_x)

    sums = g.sums
    received(cp)
    sums[:, 0:CP] = total(g.cp2, y, g.cp2r)
    received(cq)
    sums[:, CP : CP + CQ] = total(g.cq2, x, g.cq2r)
    received(lp)
    sums[:, 1152 : 1152 + LP] = total(g.lp2, y, g.lp2r)
    received(lq)
    sums[:, 1152 + LP : 1536] = total(g.lq2, x, g.lq2r)

    lane = lax.broadcasted_iota(jnp.int32, (16, LANE), 1)

    def window(base, count, start):
        t, off = start // LANE, start % LANE

        def tile(n):
            n = min(max(n, 0), count // LANE - 1)
            return sums[:, base + n * LANE : base + (n + 1) * LANE]

        if off == 0:
            return tile(t)
        return jnp.where(
            lane < LANE - off,
            pltpu.roll(tile(t), LANE - off, 1),
            pltpu.roll(tile(t + 1), LANE - off, 1),
        )

    for n in range(16):
        conv = window(0, 1152, 72 * n)
        lat = window(1152, 384, 24 * n - 72)
        g.z1[n] = jnp.where(lane < 72, conv, lat).astype(BF)
    met(2)
    zc = []
    for d in sorted(range(1, 16), key=lambda v: abs(v - 8)):
        to, t = dev_z(d)
        zc.append(send(g.z1.at[t], g.z1r.at[d - 1], to))

    received(halo)
    levels = (
        (dfx, 8, 64, 0, g.v_tf, w_fine, g.fgb, o_fine),
        (dmx, 4, 32, 64, g.v_tm, w_mid, g.mgb, o_mid),
        (dtx, 2, 16, 96, g.v_tc, w_top, g.cgb, o_coa),
    )
    for buf, h, w, at, spots, weight, out, dst in levels:
        field = buf[w : w * (h + 1)].astype(F32) + dot(spots[...], g.rs2[...])
        rows = [
            field[0:w] + g.from_n[at : at + w].astype(F32),
            field[w : w * (h - 1)],
            field[w * (h - 1) :] + g.from_s[at : at + w].astype(F32),
        ]
        whole = jnp.concatenate([part for part in rows if part.shape[0]], 0).astype(BF)
        out[...] = dot_t(whole, weight).astype(BF)
        store(out, dst)

    received(zc)
    same = g.z1[z].astype(F32)
    for d in range(15):
        same += g.z1r[d].astype(F32)
    g.z2[...] = same.astype(BF)
    received([send(g.z2, g.z2r, partner)])
    cross = g.z2r[...].astype(F32)
    first = core == 0
    both = jnp.concatenate([jnp.where(first, same, cross), jnp.where(first, cross, same)], 0)
    o_conv[...] = jnp.where(first, both[:, 0:36], pltpu.roll(both, LANE - 36, 1)[:, 0:36])
    g.turn[...] = jnp.concatenate([both, jnp.zeros((96, LANE), F32)], 0).T
    o_lat[...] = jnp.where(first, g.turn[72:84, 0:32], g.turn[84:96, 0:32])

    for copy in sent:
        copy.wait_send()
    wait(stores)


VM = pltpu.VMEM
DMA = pltpu.SemaphoreType.DMA
SCRATCH = dict(
    finx=VM((768, C), BF),
    midx=VM((256, C), BF),
    coax=VM((128, C), BF),
    coab=VM((128, C), BF),
    v_wl=VM((768, C), BF),
    v_wo=VM((2304, C), BF),
    v_cot=VM((512, C), BF),
    v_u1=VM((224, 128), BF),
    v_u2=VM((672, 256), BF),
    v_d1=VM((224, 768), BF),
    v_d2=VM((96, 256), BF),
    v_pf=VM((32, 512), BF),
    v_pm=VM((32, 128), BF),
    v_pc=VM((32, 128), BF),
    v_s1=VM((96, 128), BF),
    topb=VM((128, C), BF),
    midb=VM((256, C), BF),
    fex=VM((672, C), F32),
    shift=VM((10, 80, C), F32),
    fsh=VM((640, 768), BF),
    dsh=VM((768, 768), BF),
    shift0=VM((12, 80, C), F32),
    rims=VM((96, C), BF),
    dtx=VM((96, C), BF),
    rows_n=VM((112, C), BF),
    rows_s=VM((112, C), BF),
    from_n=VM((112, C), BF),
    from_s=VM((112, C), BF),
    cols_w=VM((48, C), BF),
    cols_e=VM((48, C), BF),
    v_rim=VM((96, 512), BF),
    v_tf=VM((512, 384), BF),
    v_tm=VM((128, 384), BF),
    v_tc=VM((32, 384), BF),
    pre=VM((512, C), F32),
    maskb=VM((512, C), BF),
    dpx=VM((512, C), BF),
    dfx=VM((768, C), BF),
    dmx=VM((256, C), BF),
    fgb=VM((512, C), BF),
    mgb=VM((128, C), BF),
    cgb=VM((32, C), BF),
    pk1=VM((32, C), BF),
    rs1=VM((128, C), BF),
    rs2=VM((384, C), BF),
    grad=VM((8, 2, 16, 2304), BF),
    got=VM((8, 16, 2304), BF),
    lgrad=VM((8, 2, 16, 768), BF),
    lgot=VM((8, 16, 768), BF),
    cp1=VM((4, 4, 16, CP), BF),
    cp1r=VM((3, 4, 16, CP), BF),
    cp2=VM((4, 16, CP), BF),
    cp2r=VM((3, 16, CP), BF),
    cq1=VM((4, 4, 16, CQ), BF),
    cq1r=VM((3, 4, 16, CQ), BF),
    cq2=VM((4, 16, CQ), BF),
    cq2r=VM((3, 16, CQ), BF),
    lp1=VM((4, 4, 16, LP), BF),
    lp1r=VM((3, 4, 16, LP), BF),
    lp2=VM((4, 16, LP), BF),
    lp2r=VM((3, 16, LP), BF),
    lq1=VM((4, 4, 16, LQ), BF),
    lq1r=VM((3, 4, 16, LQ), BF),
    lq2=VM((4, 16, LQ), BF),
    lq2r=VM((3, 16, LQ), BF),
    sums=VM((16, 1536), F32),
    z1=VM((16, 16, LANE), BF),
    z1r=VM((15, 16, LANE), BF),
    z2=VM((16, LANE), BF),
    z2r=VM((16, LANE), BF),
    far=pltpu.SemaphoreType.REGULAR((3,)),
    v_a1=VM((768, 256), BF),
    v_a2=VM((768, 128), BF),
    turn=VM((128, 128), F32),
    lsem=DMA((24,)),
    osem=DMA((4,)),
    ssem=DMA((96,)),
    rsem=DMA((96,)),
)


def hand_on(*refs):
    n = len(refs) // 3
    ins, outs, held, sems = refs[:n], refs[n : 2 * n], refs[2 * n : 3 * n], refs[3 * n]
    arrive = [pltpu.make_async_copy(ins[i], held[i], sems.at[0, i]) for i in range(n)]
    leave = [pltpu.make_async_copy(held[i], outs[i], sems.at[1, i]) for i in range(n)]
    for copy in arrive:
        copy.start()
    for i in reversed(range(n)):
        arrive[i].wait()
        leave[i].start()
    for copy in leave:
        copy.wait()


def local(consts, fine_in, mid_in, coarse_in, lateral_weight, out_weight, cotangent):
    def flat(v):
        return v.reshape(-1, v.shape[-1])

    args = [flat(fine_in), flat(mid_in), flat(coarse_in), lateral_weight, out_weight, flat(cotangent)]
    args += [jnp.asarray(v) for v in consts.values()]
    hbm = pl.BlockSpec(memory_space=pl.ANY)
    vmem = pl.BlockSpec(memory_space=pltpu.VMEM)
    outs = pl.pallas_call(
        functools.partial(kernel, tuple(consts)),
        out_shape=[
            jax.ShapeDtypeStruct((512, C), BF),
            jax.ShapeDtypeStruct((512, C), BF),
            jax.ShapeDtypeStruct((128, C), BF),
            jax.ShapeDtypeStruct((32, C), BF),
            jax.ShapeDtypeStruct((12, 32), F32),
            jax.ShapeDtypeStruct((32, 36), F32),
        ],
        in_specs=[hbm] * len(args),
        out_specs=[hbm] * 4 + [vmem] * 2,
        scratch_shapes=list(SCRATCH.values()),
        compiler_params=pltpu.CompilerParams(
            collective_id=0, has_side_effects=True, vmem_limit_bytes=63 * 2**20
        ),
        cost_estimate=pl.CostEstimate(flops=2_400_000_000, bytes_accessed=4_000_000, transcendentals=262144),
    )(*args)
    outs = pl.pallas_call(
        hand_on,
        out_shape=[jax.ShapeDtypeStruct(v.shape, v.dtype) for v in outs],
        in_specs=[hbm] * len(outs),
        out_specs=[hbm] * len(outs),
        scratch_shapes=[VM(v.shape, v.dtype) for v in outs] + [DMA((2, len(outs)))],
        compiler_params=pltpu.CompilerParams(vmem_limit_bytes=63 * 2**20),
    )(*outs)
    return (
        outs[0].reshape(fine_in.shape),
        outs[1].reshape(fine_in.shape),
        outs[2].reshape(mid_in.shape),
        outs[3].reshape(coarse_in.shape),
        outs[4],
        outs[5].T,
    )


def solution(mesh):
    field = P("rows", "cols", None)
    return jax.shard_map(
        functools.partial(local, constants()),
        mesh=mesh,
        in_specs=(field, field, field, P(), P(), field),
        out_specs=(field, field, field, field, P("cols", "rows"), P("cols", "rows")),
        check_vma=False,
    )
```

```python
import functools
from types import SimpleNamespace

import jax
import jax.numpy as jnp
import ml_dtypes
import numpy as np
from jax import lax
from jax.experimental import pallas as pl
from jax.experimental.pallas import tpu as pltpu
from jax.sharding import PartitionSpec as P

BF = jnp.bfloat16
F32 = jnp.float32
MESH = pl.DeviceIdType.MESH
C = 256
NR, NC = 8, 64
LANE = 128


def place(h, w, i, j):
    if j < 0:
        return w * (h + 2) + i + 1
    if j >= w:
        return w * (h + 2) + 16 + i + 1
    return (i + 1) * w + j


def size(h, w):
    return w * (h + 2) + 32


def cells(h, w):
    return [(i, j) for i in range(-1, h + 1) for j in range(-1, w + 1)]


def clamp(i, n, kind):
    if kind == 1:
        i = max(i, 0)
    if kind == 2:
        i = min(i, n - 1)
    return i


def up_taps(i):
    k = i // 2
    if i % 2 == 0:
        return [(k - 1, 0.25), (k, 0.75)]
    return [(k, 0.75), (k + 1, 0.25)]


def up_matrix(h, w, pad):
    mat = np.zeros((9, size(2 * h, 2 * w), pad), np.float32)
    for v in range(9):
        for i, j in cells(2 * h, 2 * w):
            for ri, rw in up_taps(i):
                for ci, cw in up_taps(j):
                    ri2, ci2 = clamp(ri, h, v // 3), clamp(ci, w, v % 3)
                    mat[v, place(2 * h, 2 * w, i, j), place(h, w, ri2, ci2)] += rw * cw
    return mat.astype(ml_dtypes.bfloat16)


def down_line(n, kind):
    line = np.zeros((n + 2, 2 * n + 4))
    for k in range(-1, n + 1):
        if (kind == 1 and k < 0) or (kind == 2 and k >= n):
            continue
        for a, weight in enumerate((0.25, 0.75, 0.75, 0.25)):
            f = clamp(2 * k - 1 + a, 2 * n, kind)
            if -2 <= f < 2 * n + 2:
                line[k + 1, f + 2] += weight
    return line


def adjoint_matrix(h, w, steps, rows, pad):
    fh, fw = h << steps, w << steps
    mat = np.zeros((9, rows, pad), np.float32)
    for v in range(9):
        lines = []
        for n, kind in ((h, v // 3), (w, v % 3)):
            line = down_line(n, kind)
            for s in range(1, steps):
                line = line[:, 1:-1] @ down_line(n << s, kind)
            lines.append(line[:, 1:-1])
        both = np.multiply.outer(*lines)
        spots = [place(fh, fw, a, b) for a, b in cells(fh, fw)]
        for i, j in cells(h, w):
            mat[v, spots, place(h, w, i, j)] = both[i + 1, :, j + 1, :].reshape(-1)
    return mat.astype(ml_dtypes.bfloat16)


def rim_matrix():
    mat = np.zeros((96, 512), np.float32)
    for a in range(3):
        for q in range(10):
            i = q - a
            if 0 <= i < 8:
                mat[16 * a + q, i * 64] = 1
                mat[48 + 16 * a + q, i * 64 + 63] = 1
    return mat.astype(ml_dtypes.bfloat16)


def scatter_matrix(h, w, level):
    mat = np.zeros((h * w, 384), np.float32)
    for side, j in ((0, 0), (1, w - 1)):
        at = 144 * side + 16 * level
        for i in range(h):
            mat[i * w + j, at + 1 + i] += 1
        mat[j, at + 48 + h + 1] += 1
        mat[(h - 1) * w + j, at + 96] += 1
    return mat.astype(ml_dtypes.bfloat16)


def pack_matrix(h, w, first, cols):
    mat = np.zeros((32, cols), np.float32)
    for i in range(h):
        mat[first + i, i * w] = 1
        mat[16 + first + i, i * w + w - 1] = 1
    return mat.astype(ml_dtypes.bfloat16)


def side_matrix(levels):
    mat = np.zeros((32 * len(levels), LANE), np.float32)
    for n, (h, first) in enumerate(levels):
        for side in range(2):
            row, src = 32 * n + 16 * side, 48 * side
            mat[row, src + 16 + first + h - 1] = 1
            for i in range(h):
                mat[row + 1 + i, src + first + i] = 1
            mat[row + 1 + h, src + 32 + first] = 1
    return mat.astype(ml_dtypes.bfloat16)


def constants():
    packs = [
        pack_matrix(8, 64, 0, 512),
        pack_matrix(4, 32, 8, 128),
        pack_matrix(2, 16, 12, 32),
    ]
    a1 = adjoint_matrix(4, 32, 1, 768, 256)
    return dict(
        u1=up_matrix(2, 16, 128),
        u2=up_matrix(4, 32, 256),
        a1=a1,
        a2=adjoint_matrix(2, 16, 2, 768, 128),
        d1=np.ascontiguousarray(a1.transpose(0, 2, 1)[:, :224]),
        d2=np.ascontiguousarray(adjoint_matrix(2, 16, 1, 256, 96).transpose(0, 2, 1)),
        pf=packs[0],
        pm=packs[1],
        pc=np.concatenate([packs[2], np.zeros((32, 96), ml_dtypes.bfloat16)], 1),
        s1=side_matrix([(8, 0), (4, 8), (2, 12)]),
        rim=rim_matrix(),
        tf=scatter_matrix(8, 64, 0),
        tm=scatter_matrix(4, 32, 1),
        tc=scatter_matrix(2, 16, 2),
    )


CP, CQ, LP, LQ = 640, 512, 128, 256


def dot(a, b):
    return jnp.dot(a, b, preferred_element_type=F32)


def dot_t(a, b):
    return lax.dot_general(a, b, (((1,), (1,)), ((), ())), preferred_element_type=F32)


def kernel(consts, *refs):
    fin, mid, coa, wl, wo_hbm, cot = refs[:6]
    k = SimpleNamespace(**dict(zip(consts, refs[6 : 6 + len(consts)])))
    o_mask, o_fine, o_mid, o_coa, o_lat, o_conv = refs[6 + len(consts) : 12 + len(consts)]
    g = SimpleNamespace(**dict(zip(SCRATCH, refs[12 + len(consts) :])))
    r, c = lax.axis_index("rows"), lax.axis_index("cols")
    y, x_lo = r // 2, r % 2
    x_hi, z, core = c // 32, (c // 2) % 16, c % 2
    x = x_hi * 2 + x_lo
    other = 1 - core
    e_n, e_s = 1 - (r + NR - 1) // NR, (r + 1) // NR
    e_w, e_e = 1 - (c + NC - 1) // NC, (c + 1) // NC
    variant = (e_n + 2 * e_s) * 3 + e_w + 2 * e_e

    up, down = (r + NR - 1) % NR, (r + 1) % NR
    left, right = (c + NC - 1) % NC, (c + 1) % NC

    def dev_x(d):
        t = (x + d) % 4
        return (y * 2 + t % 2, (t // 2) * 32 + z * 2 + core), t

    def dev_y(d):
        t = (y + d) % 4
        return (t * 2 + x_lo, c), t

    def dev_z(d):
        t = (z + d) % 16
        return (r, x_hi * 32 + t * 2 + core), t

    partner = (r, x_hi * 32 + z * 2 + other)

    peers = [(up, c), (down, c)] + [(a, b) for a in (r, up, down) for b in (left, right)]
    for d in (1, 2, 3):
        peers += [dev_x(d)[0], dev_y(d)[0]]
    peers += [dev_z(1)[0], dev_z(15)[0]]
    barrier = pltpu.get_barrier_semaphore()
    for p in peers:
        pl.semaphore_signal(barrier, inc=1, device_id=p, device_id_type=MESH)

    def greet(n):
        for d in (1 << n, 16 - (1 << n)):
            pl.semaphore_signal(g.far.at[n], inc=1, device_id=dev_z(d)[0], device_id_type=MESH)

    def met(n):
        pl.semaphore_wait(g.far.at[n], 2)

    loads = []

    def load(src, dst):
        copy = pltpu.make_async_copy(src, dst, g.lsem.at[len(loads)])
        copy.start()
        loads.append(copy)
        return copy

    inputs = [
        load(fin, g.finx.at[64:576]),
        load(mid, g.midx.at[32:160]),
        load(coa, g.coax.at[16:48]),
        load(coa, g.coab.at[0:32]),
        load(k.pf, g.v_pf),
        load(k.pm, g.v_pm),
        load(k.pc, g.v_pc),
    ]
    forward = [
        load(k.s1, g.v_s1),
        load(wl, g.v_wl),
        load(k.u1.at[variant], g.v_u1),
        load(k.u2.at[variant], g.v_u2),
    ]
    def wait(copies):
        for copy in copies:
            copy.wait()

    blank = ((g.coab, 32, 96), (g.midx, 224, 32), (g.coax, 96, 32), (g.topb, 96, 32), (g.midb, 224, 32))
    blank += ((g.finx, 672, 96), (g.dfx, 672, 96), (g.dmx, 224, 32), (g.rs1, 96, 32), (g.rs2, 288, 96))
    for ref, at, count in blank:
        ref[at : at + count] = jnp.zeros((count, C), BF)
    for at in (0, 1, 10, 11):
        g.shift0[at] = jnp.zeros((80, C), F32)
    for at in (0, 72):
        g.shift0[2:10, at : at + 8] = jnp.zeros((8, 8, C), F32)

    used = [0]

    def send(src, dst, to):
        n = used[0]
        used[0] += 1
        copy = pltpu.make_async_remote_copy(
            src_ref=src,
            dst_ref=dst,
            send_sem=g.ssem.at[n],
            recv_sem=g.rsem.at[n],
            device_id=to,
            device_id_type=MESH,
        )
        copy.start()
        return copy

    sent = []

    def received(copies):
        for copy in copies:
            copy.wait_recv()
        sent.extend(copies)

    def send_rows(buf, h, w):
        return [
            send(buf.at[w : 2 * w], buf.at[w * (h + 1) : w * (h + 2)], (up, c)),
            send(buf.at[w * h : w * (h + 1)], buf.at[0:w], (down, c)),
        ]

    def send_sides(west, east, slots):
        count = west.shape[0]

        def slot(n):
            return slots.at[count * n : count * (n + 1)]

        return [
            send(east, slot(0), (r, right)),
            send(east, slot(1), (down, right)),
            send(east, slot(2), (up, right)),
            send(west, slot(3), (r, left)),
            send(west, slot(4), (down, left)),
            send(west, slot(5), (up, left)),
        ]

    wait(inputs)
    packed = dot(g.v_pf[...], g.finx[64:576])
    packed += dot(g.v_pm[...], g.midx[32:160])
    packed += dot(g.v_pc[...], g.coab[...])
    g.pk1[...] = packed.astype(BF)
    pl.semaphore_wait(barrier, len(peers))
    halo = send_sides(g.pk1.at[0:16], g.pk1.at[16:32], g.rs1)
    halo += send_rows(g.coax, 2, 16)
    halo += send_rows(g.midx, 4, 32)
    halo += send_rows(g.finx, 8, 64)
    greet(0)
    load_wo = load(wo_hbm, g.v_wo)
    load_cot = load(cot, g.v_cot)
    adjoint = [load(k.a1.at[variant], g.v_a1), load(k.a2.at[variant], g.v_a2)]
    backward = [load(k.rim, g.v_rim)]
    closing = [
        load(k.d1.at[variant], g.v_d1),
        load(k.d2.at[variant], g.v_d2),
        load(k.tf, g.v_tf),
        load(k.tm, g.v_tm),
        load(k.tc, g.v_tc),
    ]
    wait(forward)
    wl = g.v_wl
    w_fine, w_mid, w_top = wl[0:C], wl[C : 2 * C], wl[2 * C : 3 * C]
    fex = g.fex
    fex[64:576] = dot(g.finx[64:576], w_fine)
    received(halo)
    met(0)
    greet(1)
    sides = dot(g.v_s1[...], g.rs1[...]).astype(BF)
    g.finx[640:672] = sides[0:32]
    g.midx[192:224] = sides[32:64]
    g.coax[64:96] = sides[64:96]

    g.topb[0:96] = dot(g.coax[0:96], w_top).astype(BF)
    g.midb[0:224] = (dot(g.midx[0:224], w_mid) + dot(g.v_u1[...], g.topb[...])).astype(BF)
    fex[0:64] = dot(g.finx[0:64], w_fine)
    fex[576:672] = dot(g.finx[576:672], w_fine)
    fex[...] += dot(g.v_u2[...], g.midb[...])

    keep_n, keep_s = (1 - e_n).astype(F32), (1 - e_s).astype(F32)
    keep_w, keep_e = (1 - e_w).astype(F32), (1 - e_e).astype(F32)
    line = lax.broadcasted_iota(jnp.int32, (16, C), 0)
    keep_rows = jnp.where(line == 0, keep_n, jnp.where(line == 9, keep_s, 1.0))

    def columns(s, at, out):
        for b in range(3):
            out[:, b * C : (b + 1) * C] = s[:, at[b] : at[b] + 64].astype(BF).reshape(out.shape[0], C)

    s = g.shift
    s[0, 8:72] = fex[0:64] * keep_n
    s[1:9, 8:72] = fex[64:576].reshape(8, 64, C)
    s[9, 8:72] = fex[576:640] * keep_s
    west = fex[640:656] * (keep_rows * keep_w)
    east = fex[656:672] * (keep_rows * keep_e)
    for i in range(10):
        s[i, 7:8] = west[i : i + 1]
        s[i, 72:73] = east[i : i + 1]
    columns(s, (7, 8, 9), g.fsh)

    load_wo.wait()
    wo, fsh, dsh = g.v_wo, g.fsh, g.dsh
    g.pre[...] = sum(dot(fsh[64 * a : 64 * a + 512], wo[768 * a : 768 * a + 768]) for a in range(3))
    load_cot.wait()

    def activate(q, carry):
        at = pl.multiple_of(q * 64, 64)
        v = g.pre[pl.ds(at, 64)]
        half = 0.5 + 0.5 * lax.erf(v * np.float32(np.sqrt(0.5)))
        g.maskb[pl.ds(at, 64)] = (v * half).astype(BF)
        slope = half + v * (jnp.exp(-0.5 * v * v) * np.float32(1 / np.sqrt(2 * np.pi)))
        g.dpx[pl.ds(at, 64)] = (g.v_cot[pl.ds(at, 64)].astype(F32) * slope).astype(BF)
        return carry

    lax.fori_loop(0, 8, activate, 0)
    stores = []

    def store(src, dst):
        copy = pltpu.make_async_copy(src, dst, g.osem.at[len(stores)])
        copy.start()
        stores.append(copy)

    store(g.maskb, o_mask)

    grad, got = g.grad, g.got
    dpre_t = g.dpx[...].T
    pair = []
    for a in range(3):
        lanes = pl.ds(768 * a, 768)
        term = dot(dpre_t, fsh[64 * a : 64 * a + 512]).astype(BF)
        grad[:, :, :, lanes] = term.reshape(8, 2, 16, 768)
        pair.append(send(grad.at[:, other, :, lanes], got.at[:, :, lanes], partner))

    def begin(buf, slots, dev):
        out = []
        for d in (1, 2, 3):
            to, t = dev(d)
            out.append(send(buf.at[t], slots.at[d - 1], to))
        return out

    def total(buf, mine, slots):
        return buf[mine].astype(F32) + slots[0].astype(F32) + slots[1].astype(F32) + slots[2].astype(F32)

    def split(mine, theirs, half, p, q):
        wp, wq = p.shape[-1], q.shape[-1]
        for n in range(8):
            part = (mine[n, core].astype(F32) + theirs[n].astype(F32)).astype(BF)
            for h in range(2):
                at = half * h
                p[2 * h + n % 2, n // 2] = part[:, at : at + wp]
                q[n // 2, 2 * h + n % 2] = part[:, at + wp : at + wp + wq]

    s = g.shift0
    s[2:10, 8:72] = g.dpx[...].astype(F32).reshape(8, 64, C)
    columns(s, (9, 8, 7), dsh)
    wait(backward)
    g.rims[...] = dot(g.v_rim[...], g.dpx[...]).astype(BF)
    body = west = east = None
    for a in range(3):
        for b in range(3):
            block = wo[(3 * a + b) * C : (3 * a + b + 1) * C]
            term = dot_t(dsh[64 * (2 - a) : 64 * (2 - a) + 640, b * C : (b + 1) * C], block)
            body = term if body is None else body + term
            if b == 0:
                term = dot_t(g.rims[16 * a : 16 * a + 16], block)
                west = term if west is None else west + term
            if b == 2:
                term = dot_t(g.rims[48 + 16 * a : 64 + 16 * a], block)
                east = term if east is None else east + term
    dfx = g.dfx
    dfx[0:64] = (body[0:64] * keep_n).astype(BF)
    dfx[64:576] = body[64:576].astype(BF)
    dfx[576:640] = (body[576:640] * keep_s).astype(BF)
    dfx[640:656] = (west * (keep_rows * keep_w)).astype(BF)
    dfx[656:672] = (east * (keep_rows * keep_e)).astype(BF)

    received(pair)
    split(grad, got, 1152, g.cp1, g.cq1)
    cp = begin(g.cp1, g.cp1r, dev_x)
    cq = begin(g.cq1, g.cq1r, dev_y)
    met(1)
    greet(2)

    lgrad, lgot = g.lgrad, g.lgot
    wait(adjoint)
    dfine_t = dfx[...].T
    lpair = []
    for n in range(3):
        lanes = pl.ds(n * C, C)
        if n == 0:
            rows = g.finx[...]
        elif n == 1:
            rows = dot(g.v_a1[...], g.midx[...]).astype(BF)
        else:
            rows = dot(g.v_a2[...], g.coax[...]).astype(BF)
        lgrad[:, :, :, lanes] = dot(dfine_t, rows).astype(BF).reshape(8, 2, 16, C)
        lpair.append(send(lgrad.at[:, other, :, lanes], lgot.at[:, :, lanes], partner))

    received(lpair)
    split(lgrad, lgot, 384, g.lp1, g.lq1)
    lp = begin(g.lp1, g.lp1r, dev_x)
    lq = begin(g.lq1, g.lq1r, dev_y)

    wait(closing)
    dmx, dtx = g.dmx, g.dtx
    dmx[0:224] = dot(g.v_d1[...], dfx[...]).astype(BF)
    dtx[...] = dot(g.v_d2[...], dmx[...]).astype(BF)
    north, south, west, east = g.rows_n, g.rows_s, g.cols_w, g.cols_e
    for n, (buf, h, w, at) in enumerate(((dfx, 8, 64, 0), (dmx, 4, 32, 64), (dtx, 2, 16, 96))):
        north[at : at + w] = buf[0:w]
        south[at : at + w] = buf[w * (h + 1) : w * (h + 2)]
        west[16 * n : 16 * n + 16] = buf[w * (h + 2) : w * (h + 2) + 16]
        east[16 * n : 16 * n + 16] = buf[w * (h + 2) + 16 : w * (h + 2) + 32]
    received(cp)
    g.cp2[...] = total(g.cp1, x, g.cp1r).astype(BF)
    cp = begin(g.cp2, g.cp2r, dev_y)
    received(cq)
    g.cq2[...] = total(g.cq1, y, g.cq1r).astype(BF)
    cq = begin(g.cq2, g.cq2r, dev_x)

    received(lp)
    g.lp2[...] = total(g.lp1, x, g.lp1r).astype(BF)
    lp = begin(g.lp2, g.lp2r, dev_y)
    received(lq)
    g.lq2[...] = total(g.lq1, y, g.lq1r).astype(BF)
    lq = begin(g.lq2, g.lq2r, dev_x)

    sums = g.sums
    received(cp)
    sums[:, 0:CP] = total(g.cp2, y, g.cp2r)
    received(cq)
    sums[:, CP : CP + CQ] = total(g.cq2, x, g.cq2r)
    received(lp)
    sums[:, 1152 : 1152 + LP] = total(g.lp2, y, g.lp2r)
    received(lq)
    sums[:, 1152 + LP : 1536] = total(g.lq2, x, g.lq2r)

    lane = lax.broadcasted_iota(jnp.int32, (16, LANE), 1)

    def window(base, count, start):
        t, off = start // LANE, start % LANE

        def tile(n):
            n = min(max(n, 0), count // LANE - 1)
            return sums[:, base + n * LANE : base + (n + 1) * LANE]

        if off == 0:
            return tile(t)
        return jnp.where(
            lane < LANE - off,
            pltpu.roll(tile(t), LANE - off, 1),
            pltpu.roll(tile(t + 1), LANE - off, 1),
        )

    for n in range(16):
        conv = window(0, 1152, 72 * n)
        lat = window(1152, 384, 24 * n - 72)
        g.z1[n] = jnp.where(lane < 72, conv, lat).astype(BF)
    met(2)
    zc = []
    for d in sorted(range(1, 16), key=lambda v: abs(v - 8)):
        to, t = dev_z(d)
        zc.append(send(g.z1.at[t], g.z1r.at[d - 1], to))

    halo = send_sides(west, east, g.rs2)
    halo += [send(north, g.from_s, (up, c)), send(south, g.from_n, (down, c))]

    received(zc)
    same = g.z1[z].astype(F32)
    for d in range(15):
        same += g.z1r[d].astype(F32)
    g.z2[...] = same.astype(BF)
    swap = [send(g.z2, g.z2r, partner)]
    received(halo)
    levels = (
        (dfx, 8, 64, 0, g.v_tf, w_fine, g.fgb, o_fine),
        (dmx, 4, 32, 64, g.v_tm, w_mid, g.mgb, o_mid),
        (dtx, 2, 16, 96, g.v_tc, w_top, g.cgb, o_coa),
    )
    for buf, h, w, at, spots, weight, out, dst in levels:
        field = buf[w : w * (h + 1)].astype(F32) + dot(spots[...], g.rs2[...])
        rows = [
            field[0:w] + g.from_n[at : at + w].astype(F32),
            field[w : w * (h - 1)],
            field[w * (h - 1) :] + g.from_s[at : at + w].astype(F32),
        ]
        whole = jnp.concatenate([part for part in rows if part.shape[0]], 0).astype(BF)
        out[...] = dot_t(whole, weight).astype(BF)
        store(out, dst)

    received(swap)
    cross = g.z2r[...].astype(F32)
    first = core == 0
    both = jnp.concatenate([jnp.where(first, same, cross), jnp.where(first, cross, same)], 0)
    o_conv[...] = jnp.where(first, both[:, 0:36], pltpu.roll(both, LANE - 36, 1)[:, 0:36])
    g.turn[...] = jnp.concatenate([both, jnp.zeros((96, LANE), F32)], 0).T
    o_lat[...] = jnp.where(first, g.turn[72:84, 0:32], g.turn[84:96, 0:32])

    for copy in sent:
        copy.wait_send()
    wait(stores)


VM = pltpu.VMEM
DMA = pltpu.SemaphoreType.DMA
SCRATCH = dict(
    finx=VM((768, C), BF),
    midx=VM((256, C), BF),
    coax=VM((128, C), BF),
    coab=VM((128, C), BF),
    v_wl=VM((768, C), BF),
    v_wo=VM((2304, C), BF),
    v_cot=VM((512, C), BF),
    v_u1=VM((224, 128), BF),
    v_u2=VM((672, 256), BF),
    v_d1=VM((224, 768), BF),
    v_d2=VM((96, 256), BF),
    v_pf=VM((32, 512), BF),
    v_pm=VM((32, 128), BF),
    v_pc=VM((32, 128), BF),
    v_s1=VM((96, 128), BF),
    topb=VM((128, C), BF),
    midb=VM((256, C), BF),
    fex=VM((672, C), F32),
    shift=VM((10, 80, C), F32),
    fsh=VM((640, 768), BF),
    dsh=VM((768, 768), BF),
    shift0=VM((12, 80, C), F32),
    rims=VM((96, C), BF),
    dtx=VM((96, C), BF),
    rows_n=VM((112, C), BF),
    rows_s=VM((112, C), BF),
    from_n=VM((112, C), BF),
    from_s=VM((112, C), BF),
    cols_w=VM((48, C), BF),
    cols_e=VM((48, C), BF),
    v_rim=VM((96, 512), BF),
    v_tf=VM((512, 384), BF),
    v_tm=VM((128, 384), BF),
    v_tc=VM((32, 384), BF),
    pre=VM((512, C), F32),
    maskb=VM((512, C), BF),
    dpx=VM((512, C), BF),
    dfx=VM((768, C), BF),
    dmx=VM((256, C), BF),
    fgb=VM((512, C), BF),
    mgb=VM((128, C), BF),
    cgb=VM((32, C), BF),
    pk1=VM((32, C), BF),
    rs1=VM((128, C), BF),
    rs2=VM((384, C), BF),
    grad=VM((8, 2, 16, 2304), BF),
    got=VM((8, 16, 2304), BF),
    lgrad=VM((8, 2, 16, 768), BF),
    lgot=VM((8, 16, 768), BF),
    cp1=VM((4, 4, 16, CP), BF),
    cp1r=VM((3, 4, 16, CP), BF),
    cp2=VM((4, 16, CP), BF),
    cp2r=VM((3, 16, CP), BF),
    cq1=VM((4, 4, 16, CQ), BF),
    cq1r=VM((3, 4, 16, CQ), BF),
    cq2=VM((4, 16, CQ), BF),
    cq2r=VM((3, 16, CQ), BF),
    lp1=VM((4, 4, 16, LP), BF),
    lp1r=VM((3, 4, 16, LP), BF),
    lp2=VM((4, 16, LP), BF),
    lp2r=VM((3, 16, LP), BF),
    lq1=VM((4, 4, 16, LQ), BF),
    lq1r=VM((3, 4, 16, LQ), BF),
    lq2=VM((4, 16, LQ), BF),
    lq2r=VM((3, 16, LQ), BF),
    sums=VM((16, 1536), F32),
    z1=VM((16, 16, LANE), BF),
    z1r=VM((15, 16, LANE), BF),
    z2=VM((16, LANE), BF),
    z2r=VM((16, LANE), BF),
    far=pltpu.SemaphoreType.REGULAR((3,)),
    v_a1=VM((768, 256), BF),
    v_a2=VM((768, 128), BF),
    turn=VM((128, 128), F32),
    lsem=DMA((24,)),
    osem=DMA((4,)),
    ssem=DMA((96,)),
    rsem=DMA((96,)),
)


def hand_on(*refs):
    n = len(refs) // 3
    ins, outs, held, sems = refs[:n], refs[n : 2 * n], refs[2 * n : 3 * n], refs[3 * n]
    arrive = [pltpu.make_async_copy(ins[i], held[i], sems.at[0, i]) for i in range(n)]
    leave = [pltpu.make_async_copy(held[i], outs[i], sems.at[1, i]) for i in range(n)]
    for copy in arrive:
        copy.start()
    for i in reversed(range(n)):
        arrive[i].wait()
        leave[i].start()
    for copy in leave:
        copy.wait()


def local(consts, fine_in, mid_in, coarse_in, lateral_weight, out_weight, cotangent):
    def flat(v):
        return v.reshape(-1, v.shape[-1])

    args = [flat(fine_in), flat(mid_in), flat(coarse_in), lateral_weight, out_weight, flat(cotangent)]
    args += [jnp.asarray(v) for v in consts.values()]
    hbm = pl.BlockSpec(memory_space=pl.ANY)
    vmem = pl.BlockSpec(memory_space=pltpu.VMEM)
    outs = pl.pallas_call(
        functools.partial(kernel, tuple(consts)),
        out_shape=[
            jax.ShapeDtypeStruct((512, C), BF),
            jax.ShapeDtypeStruct((512, C), BF),
            jax.ShapeDtypeStruct((128, C), BF),
            jax.ShapeDtypeStruct((32, C), BF),
            jax.ShapeDtypeStruct((12, 32), F32),
            jax.ShapeDtypeStruct((32, 36), F32),
        ],
        in_specs=[hbm] * len(args),
        out_specs=[hbm] * 4 + [vmem] * 2,
        scratch_shapes=list(SCRATCH.values()),
        compiler_params=pltpu.CompilerParams(
            collective_id=0, has_side_effects=True, vmem_limit_bytes=63 * 2**20
        ),
        cost_estimate=pl.CostEstimate(flops=2_400_000_000, bytes_accessed=4_000_000, transcendentals=262144),
    )(*args)
    outs = pl.pallas_call(
        hand_on,
        out_shape=[jax.ShapeDtypeStruct(v.shape, v.dtype) for v in outs],
        in_specs=[hbm] * len(outs),
        out_specs=[hbm] * len(outs),
        scratch_shapes=[VM(v.shape, v.dtype) for v in outs] + [DMA((2, len(outs)))],
        compiler_params=pltpu.CompilerParams(vmem_limit_bytes=63 * 2**20),
    )(*outs)
    return (
        outs[0].reshape(fine_in.shape),
        outs[1].reshape(fine_in.shape),
        outs[2].reshape(mid_in.shape),
        outs[3].reshape(coarse_in.shape),
        outs[4],
        outs[5].T,
    )


def solution(mesh):
    field = P("rows", "cols", None)
    return jax.shard_map(
        functools.partial(local, constants()),
        mesh=mesh,
        in_specs=(field, field, field, P(), P(), field),
        out_specs=(field, field, field, field, P("cols", "rows"), P("cols", "rows")),
        check_vma=False,
    )
```

```python
import functools
from types import SimpleNamespace

import jax
import jax.numpy as jnp
import ml_dtypes
import numpy as np
from jax import lax
from jax.experimental import pallas as pl
from jax.experimental.pallas import tpu as pltpu
from jax.sharding import PartitionSpec as P

BF = jnp.bfloat16
F32 = jnp.float32
MESH = pl.DeviceIdType.MESH
C = 256
NR, NC = 8, 64
LANE = 128


def place(h, w, i, j):
    if j < 0:
        return w * (h + 2) + i + 1
    if j >= w:
        return w * (h + 2) + 16 + i + 1
    return (i + 1) * w + j


def size(h, w):
    return w * (h + 2) + 32


def cells(h, w):
    return [(i, j) for i in range(-1, h + 1) for j in range(-1, w + 1)]


def clamp(i, n, kind):
    if kind == 1:
        i = max(i, 0)
    if kind == 2:
        i = min(i, n - 1)
    return i


def up_taps(i):
    k = i // 2
    if i % 2 == 0:
        return [(k - 1, 0.25), (k, 0.75)]
    return [(k, 0.75), (k + 1, 0.25)]


def up_matrix(h, w, pad):
    mat = np.zeros((9, size(2 * h, 2 * w), pad), np.float32)
    for v in range(9):
        for i, j in cells(2 * h, 2 * w):
            for ri, rw in up_taps(i):
                for ci, cw in up_taps(j):
                    ri2, ci2 = clamp(ri, h, v // 3), clamp(ci, w, v % 3)
                    mat[v, place(2 * h, 2 * w, i, j), place(h, w, ri2, ci2)] += rw * cw
    return mat.astype(ml_dtypes.bfloat16)


def down_line(n, kind):
    line = np.zeros((n + 2, 2 * n + 4))
    for k in range(-1, n + 1):
        if (kind == 1 and k < 0) or (kind == 2 and k >= n):
            continue
        for a, weight in enumerate((0.25, 0.75, 0.75, 0.25)):
            f = clamp(2 * k - 1 + a, 2 * n, kind)
            if -2 <= f < 2 * n + 2:
                line[k + 1, f + 2] += weight
    return line


def adjoint_matrix(h, w, steps, rows, pad):
    fh, fw = h << steps, w << steps
    mat = np.zeros((9, rows, pad), np.float32)
    for v in range(9):
        lines = []
        for n, kind in ((h, v // 3), (w, v % 3)):
            line = down_line(n, kind)
            for s in range(1, steps):
                line = line[:, 1:-1] @ down_line(n << s, kind)
            lines.append(line[:, 1:-1])
        both = np.multiply.outer(*lines)
        spots = [place(fh, fw, a, b) for a, b in cells(fh, fw)]
        for i, j in cells(h, w):
            mat[v, spots, place(h, w, i, j)] = both[i + 1, :, j + 1, :].reshape(-1)
    return mat.astype(ml_dtypes.bfloat16)


def rim_matrix():
    mat = np.zeros((96, 512), np.float32)
    for a in range(3):
        for q in range(10):
            i = q - a
            if 0 <= i < 8:
                mat[16 * a + q, i * 64] = 1
                mat[48 + 16 * a + q, i * 64 + 63] = 1
    return mat.astype(ml_dtypes.bfloat16)


def scatter_matrix(h, w, level):
    mat = np.zeros((h * w, 384), np.float32)
    for side, j in ((0, 0), (1, w - 1)):
        at = 144 * side + 16 * level
        for i in range(h):
            mat[i * w + j, at + 1 + i] += 1
        mat[j, at + 48 + h + 1] += 1
        mat[(h - 1) * w + j, at + 96] += 1
    return mat.astype(ml_dtypes.bfloat16)


def pack_matrix(h, w, first, cols):
    mat = np.zeros((32, cols), np.float32)
    for i in range(h):
        mat[first + i, i * w] = 1
        mat[16 + first + i, i * w + w - 1] = 1
    return mat.astype(ml_dtypes.bfloat16)


def side_matrix(levels):
    mat = np.zeros((32 * len(levels), LANE), np.float32)
    for n, (h, first) in enumerate(levels):
        for side in range(2):
            row, src = 32 * n + 16 * side, 48 * side
            mat[row, src + 16 + first + h - 1] = 1
            for i in range(h):
                mat[row + 1 + i, src + first + i] = 1
            mat[row + 1 + h, src + 32 + first] = 1
    return mat.astype(ml_dtypes.bfloat16)


def constants():
    packs = [
        pack_matrix(8, 64, 0, 512),
        pack_matrix(4, 32, 8, 128),
        pack_matrix(2, 16, 12, 32),
    ]
    a1 = adjoint_matrix(4, 32, 1, 768, 256)
    return dict(
        u1=up_matrix(2, 16, 128),
        u2=up_matrix(4, 32, 256),
        a1=a1,
        a2=adjoint_matrix(2, 16, 2, 768, 128),
        d1=np.ascontiguousarray(a1.transpose(0, 2, 1)[:, :224]),
        d2=np.ascontiguousarray(adjoint_matrix(2, 16, 1, 256, 96).transpose(0, 2, 1)),
        pf=packs[0],
        pm=packs[1],
        pc=np.concatenate([packs[2], np.zeros((32, 96), ml_dtypes.bfloat16)], 1),
        s1=side_matrix([(8, 0), (4, 8), (2, 12)]),
        rim=rim_matrix(),
        tf=scatter_matrix(8, 64, 0),
        tm=scatter_matrix(4, 32, 1),
        tc=scatter_matrix(2, 16, 2),
    )


CP, CQ, LP, LQ = 640, 512, 128, 256


def dot(a, b):
    return jnp.dot(a, b, preferred_element_type=F32)


def dot_t(a, b):
    return lax.dot_general(a, b, (((1,), (1,)), ((), ())), preferred_element_type=F32)


def kernel(consts, *refs):
    fin, mid, coa, wl, wo_hbm, cot = refs[:6]
    k = SimpleNamespace(**dict(zip(consts, refs[6 : 6 + len(consts)])))
    o_mask, o_fine, o_mid, o_coa, o_lat, o_conv = refs[6 + len(consts) : 12 + len(consts)]
    g = SimpleNamespace(**dict(zip(SCRATCH, refs[12 + len(consts) :])))
    r, c = lax.axis_index("rows"), lax.axis_index("cols")
    y, x_lo = r // 2, r % 2
    x_hi, z, core = c // 32, (c // 2) % 16, c % 2
    x = x_hi * 2 + x_lo
    other = 1 - core
    e_n, e_s = 1 - (r + NR - 1) // NR, (r + 1) // NR
    e_w, e_e = 1 - (c + NC - 1) // NC, (c + 1) // NC
    variant = (e_n + 2 * e_s) * 3 + e_w + 2 * e_e

    up, down = (r + NR - 1) % NR, (r + 1) % NR
    left, right = (c + NC - 1) % NC, (c + 1) % NC

    def dev_x(d):
        t = (x + d) % 4
        return (y * 2 + t % 2, (t // 2) * 32 + z * 2 + core), t

    def dev_y(d):
        t = (y + d) % 4
        return (t * 2 + x_lo, c), t

    def dev_z(d):
        t = (z + d) % 16
        return (r, x_hi * 32 + t * 2 + core), t

    partner = (r, x_hi * 32 + z * 2 + other)

    peers = [(a, b) for a in (up, down, r) for b in (left, right)] + [(up, c), (down, c)]
    for d in (1, 2, 3):
        peers += [dev_x(d)[0], dev_y(d)[0]]
    peers += [dev_z(1)[0], dev_z(15)[0]]
    barrier = pltpu.get_barrier_semaphore()
    for p in peers:
        pl.semaphore_signal(barrier, inc=1, device_id=p, device_id_type=MESH)

    def greet(n):
        for d in (1 << n, 16 - (1 << n)):
            pl.semaphore_signal(g.far.at[n], inc=1, device_id=dev_z(d)[0], device_id_type=MESH)

    def met(n):
        pl.semaphore_wait(g.far.at[n], 2)

    loads = []

    def load(src, dst):
        copy = pltpu.make_async_copy(src, dst, g.lsem.at[len(loads)])
        copy.start()
        loads.append(copy)
        return copy

    inputs = [
        load(fin, g.finx.at[64:576]),
        load(mid, g.midx.at[32:160]),
        load(coa, g.coax.at[16:48]),
        load(coa, g.coab.at[0:32]),
        load(k.pf, g.v_pf),
        load(k.pm, g.v_pm),
        load(k.pc, g.v_pc),
    ]
    forward = [
        load(k.s1, g.v_s1),
        load(wl, g.v_wl),
        load(k.u1.at[variant], g.v_u1),
        load(k.u2.at[variant], g.v_u2),
    ]
    def wait(copies):
        for copy in copies:
            copy.wait()

    blank = ((g.coab, 32, 96), (g.midx, 224, 32), (g.coax, 96, 32), (g.topb, 96, 32), (g.midb, 224, 32))
    blank += ((g.finx, 672, 96), (g.dfx, 672, 96), (g.dmx, 224, 32), (g.rs1, 96, 32), (g.rs2, 288, 96))
    for ref, at, count in blank:
        ref[at : at + count] = jnp.zeros((count, C), BF)
    for at in (0, 1, 10, 11):
        g.shift0[at] = jnp.zeros((80, C), F32)
    for at in (0, 72):
        g.shift0[2:10, at : at + 8] = jnp.zeros((8, 8, C), F32)

    used = [0]

    def send(src, dst, to):
        n = used[0]
        used[0] += 1
        copy = pltpu.make_async_remote_copy(
            src_ref=src,
            dst_ref=dst,
            send_sem=g.ssem.at[n],
            recv_sem=g.rsem.at[n],
            device_id=to,
            device_id_type=MESH,
        )
        copy.start()
        return copy

    sent = []

    def received(copies):
        for copy in copies:
            copy.wait_recv()
        sent.extend(copies)

    def send_rows(buf, h, w):
        return [
            send(buf.at[w : 2 * w], buf.at[w * (h + 1) : w * (h + 2)], (up, c)),
            send(buf.at[w * h : w * (h + 1)], buf.at[0:w], (down, c)),
        ]

    def send_sides(west, east, slots):
        count = west.shape[0]

        def slot(n):
            return slots.at[count * n : count * (n + 1)]

        return [
            send(east, slot(1), (down, right)),
            send(east, slot(2), (up, right)),
            send(west, slot(4), (down, left)),
            send(west, slot(5), (up, left)),
            send(east, slot(0), (r, right)),
            send(west, slot(3), (r, left)),
        ]

    wait(inputs)
    packed = dot(g.v_pf[...], g.finx[64:576])
    packed += dot(g.v_pm[...], g.midx[32:160])
    packed += dot(g.v_pc[...], g.coab[...])
    g.pk1[...] = packed.astype(BF)
    pl.semaphore_wait(barrier, len(peers))
    halo = send_sides(g.pk1.at[0:16], g.pk1.at[16:32], g.rs1)
    halo += send_rows(g.coax, 2, 16)
    halo += send_rows(g.midx, 4, 32)
    halo += send_rows(g.finx, 8, 64)
    greet(0)
    load_wo = load(wo_hbm, g.v_wo)
    load_cot = load(cot, g.v_cot)
    adjoint = [load(k.a1.at[variant], g.v_a1), load(k.a2.at[variant], g.v_a2)]
    backward = [load(k.rim, g.v_rim)]
    closing = [
        load(k.d1.at[variant], g.v_d1),
        load(k.d2.at[variant], g.v_d2),
        load(k.tf, g.v_tf),
        load(k.tm, g.v_tm),
        load(k.tc, g.v_tc),
    ]
    wait(forward)
    wl = g.v_wl
    w_fine, w_mid, w_top = wl[0:C], wl[C : 2 * C], wl[2 * C : 3 * C]
    fex = g.fex
    fex[64:576] = dot(g.finx[64:576], w_fine)
    received(halo)
    met(0)
    greet(1)
    sides = dot(g.v_s1[...], g.rs1[...]).astype(BF)
    g.finx[640:672] = sides[0:32]
    g.midx[192:224] = sides[32:64]
    g.coax[64:96] = sides[64:96]

    g.topb[0:96] = dot(g.coax[0:96], w_top).astype(BF)
    g.midb[0:224] = (dot(g.midx[0:224], w_mid) + dot(g.v_u1[...], g.topb[...])).astype(BF)
    fex[0:64] = dot(g.finx[0:64], w_fine)
    fex[576:672] = dot(g.finx[576:672], w_fine)
    fex[...] += dot(g.v_u2[...], g.midb[...])

    keep_n, keep_s = (1 - e_n).astype(F32), (1 - e_s).astype(F32)
    keep_w, keep_e = (1 - e_w).astype(F32), (1 - e_e).astype(F32)
    line = lax.broadcasted_iota(jnp.int32, (16, C), 0)
    keep_rows = jnp.where(line == 0, keep_n, jnp.where(line == 9, keep_s, 1.0))

    def columns(s, at, out):
        for b in range(3):
            out[:, b * C : (b + 1) * C] = s[:, at[b] : at[b] + 64].astype(BF).reshape(out.shape[0], C)

    s = g.shift
    s[0, 8:72] = fex[0:64] * keep_n
    s[1:9, 8:72] = fex[64:576].reshape(8, 64, C)
    s[9, 8:72] = fex[576:640] * keep_s
    west = fex[640:656] * (keep_rows * keep_w)
    east = fex[656:672] * (keep_rows * keep_e)
    for i in range(10):
        s[i, 7:8] = west[i : i + 1]
        s[i, 72:73] = east[i : i + 1]
    columns(s, (7, 8, 9), g.fsh)

    load_wo.wait()
    wo, fsh, dsh = g.v_wo, g.fsh, g.dsh
    g.pre[...] = sum(dot(fsh[64 * a : 64 * a + 512], wo[768 * a : 768 * a + 768]) for a in range(3))
    load_cot.wait()

    def activate(q, carry):
        at = pl.multiple_of(q * 64, 64)
        v = g.pre[pl.ds(at, 64)]
        half = 0.5 + 0.5 * lax.erf(v * np.float32(np.sqrt(0.5)))
        g.maskb[pl.ds(at, 64)] = (v * half).astype(BF)
        slope = half + v * (jnp.exp(-0.5 * v * v) * np.float32(1 / np.sqrt(2 * np.pi)))
        g.dpx[pl.ds(at, 64)] = (g.v_cot[pl.ds(at, 64)].astype(F32) * slope).astype(BF)
        return carry

    lax.fori_loop(0, 8, activate, 0)
    stores = []

    def store(src, dst):
        copy = pltpu.make_async_copy(src, dst, g.osem.at[len(stores)])
        copy.start()
        stores.append(copy)

    store(g.maskb, o_mask)

    grad, got = g.grad, g.got
    dpre_t = g.dpx[...].T
    pair = []
    for a in range(3):
        lanes = pl.ds(768 * a, 768)
        term = dot(dpre_t, fsh[64 * a : 64 * a + 512]).astype(BF)
        grad[:, :, :, lanes] = term.reshape(8, 2, 16, 768)
        pair.append(send(grad.at[:, other, :, lanes], got.at[:, :, lanes], partner))

    def begin(buf, slots, dev):
        out = []
        for d in (1, 2, 3):
            to, t = dev(d)
            out.append(send(buf.at[t], slots.at[d - 1], to))
        return out

    def total(buf, mine, slots):
        return buf[mine].astype(F32) + slots[0].astype(F32) + slots[1].astype(F32) + slots[2].astype(F32)

    def split(mine, theirs, half, p, q):
        wp, wq = p.shape[-1], q.shape[-1]
        for n in range(8):
            part = (mine[n, core].astype(F32) + theirs[n].astype(F32)).astype(BF)
            for h in range(2):
                at = half * h
                p[2 * h + n % 2, n // 2] = part[:, at : at + wp]
                q[n // 2, 2 * h + n % 2] = part[:, at + wp : at + wp + wq]

    s = g.shift0
    s[2:10, 8:72] = g.dpx[...].astype(F32).reshape(8, 64, C)
    columns(s, (9, 8, 7), dsh)
    wait(backward)
    g.rims[...] = dot(g.v_rim[...], g.dpx[...]).astype(BF)
    body = west = east = None
    for a in range(3):
        for b in range(3):
            block = wo[(3 * a + b) * C : (3 * a + b + 1) * C]
            term = dot_t(dsh[64 * (2 - a) : 64 * (2 - a) + 640, b * C : (b + 1) * C], block)
            body = term if body is None else body + term
            if b == 0:
                term = dot_t(g.rims[16 * a : 16 * a + 16], block)
                west = term if west is None else west + term
            if b == 2:
                term = dot_t(g.rims[48 + 16 * a : 64 + 16 * a], block)
                east = term if east is None else east + term
    dfx = g.dfx
    dfx[0:64] = (body[0:64] * keep_n).astype(BF)
    dfx[64:576] = body[64:576].astype(BF)
    dfx[576:640] = (body[576:640] * keep_s).astype(BF)
    dfx[640:656] = (west * (keep_rows * keep_w)).astype(BF)
    dfx[656:672] = (east * (keep_rows * keep_e)).astype(BF)

    received(pair)
    split(grad, got, 1152, g.cp1, g.cq1)
    cp = begin(g.cp1, g.cp1r, dev_x)
    cq = begin(g.cq1, g.cq1r, dev_y)
    met(1)
    greet(2)

    lgrad, lgot = g.lgrad, g.lgot
    wait(adjoint)
    dfine_t = dfx[...].T
    lpair = []
    for n in range(3):
        lanes = pl.ds(n * C, C)
        if n == 0:
            rows = g.finx[...]
        elif n == 1:
            rows = dot(g.v_a1[...], g.midx[...]).astype(BF)
        else:
            rows = dot(g.v_a2[...], g.coax[...]).astype(BF)
        lgrad[:, :, :, lanes] = dot(dfine_t, rows).astype(BF).reshape(8, 2, 16, C)
        lpair.append(send(lgrad.at[:, other, :, lanes], lgot.at[:, :, lanes], partner))

    received(lpair)
    split(lgrad, lgot, 384, g.lp1, g.lq1)
    lp = begin(g.lp1, g.lp1r, dev_x)
    lq = begin(g.lq1, g.lq1r, dev_y)

    wait(closing)
    dmx, dtx = g.dmx, g.dtx
    dmx[0:224] = dot(g.v_d1[...], dfx[...]).astype(BF)
    dtx[...] = dot(g.v_d2[...], dmx[...]).astype(BF)
    north, south, west, east = g.rows_n, g.rows_s, g.cols_w, g.cols_e
    for n, (buf, h, w, at) in enumerate(((dfx, 8, 64, 0), (dmx, 4, 32, 64), (dtx, 2, 16, 96))):
        north[at : at + w] = buf[0:w]
        south[at : at + w] = buf[w * (h + 1) : w * (h + 2)]
        west[16 * n : 16 * n + 16] = buf[w * (h + 2) : w * (h + 2) + 16]
        east[16 * n : 16 * n + 16] = buf[w * (h + 2) + 16 : w * (h + 2) + 32]
    received(cp)
    g.cp2[...] = total(g.cp1, x, g.cp1r).astype(BF)
    cp = begin(g.cp2, g.cp2r, dev_y)
    received(cq)
    g.cq2[...] = total(g.cq1, y, g.cq1r).astype(BF)
    cq = begin(g.cq2, g.cq2r, dev_x)

    received(lp)
    g.lp2[...] = total(g.lp1, x, g.lp1r).astype(BF)
    lp = begin(g.lp2, g.lp2r, dev_y)
    received(lq)
    g.lq2[...] = total(g.lq1, y, g.lq1r).astype(BF)
    lq = begin(g.lq2, g.lq2r, dev_x)

    sums = g.sums
    received(cp)
    sums[:, 0:CP] = total(g.cp2, y, g.cp2r)
    received(cq)
    sums[:, CP : CP + CQ] = total(g.cq2, x, g.cq2r)
    received(lp)
    sums[:, 1152 : 1152 + LP] = total(g.lp2, y, g.lp2r)
    received(lq)
    sums[:, 1152 + LP : 1536] = total(g.lq2, x, g.lq2r)

    lane = lax.broadcasted_iota(jnp.int32, (16, LANE), 1)

    def window(base, count, start):
        t, off = start // LANE, start % LANE

        def tile(n):
            n = min(max(n, 0), count // LANE - 1)
            return sums[:, base + n * LANE : base + (n + 1) * LANE]

        if off == 0:
            return tile(t)
        return jnp.where(
            lane < LANE - off,
            pltpu.roll(tile(t), LANE - off, 1),
            pltpu.roll(tile(t + 1), LANE - off, 1),
        )

    for n in range(16):
        conv = window(0, 1152, 72 * n)
        lat = window(1152, 384, 24 * n - 72)
        g.z1[n] = jnp.where(lane < 72, conv, lat).astype(BF)
    met(2)
    zc = []
    for d in sorted(range(1, 16), key=lambda v: abs(v - 8)):
        to, t = dev_z(d)
        zc.append(send(g.z1.at[t], g.z1r.at[d - 1], to))

    halo = send_sides(west, east, g.rs2)
    halo += [send(north, g.from_s, (up, c)), send(south, g.from_n, (down, c))]

    received(zc)
    same = g.z1[z].astype(F32)
    for d in range(15):
        same += g.z1r[d].astype(F32)
    g.z2[...] = same.astype(BF)
    swap = [send(g.z2, g.z2r, partner)]
    received(halo)
    levels = (
        (dfx, 8, 64, 0, g.v_tf, w_fine, g.fgb, o_fine),
        (dmx, 4, 32, 64, g.v_tm, w_mid, g.mgb, o_mid),
        (dtx, 2, 16, 96, g.v_tc, w_top, g.cgb, o_coa),
    )
    for buf, h, w, at, spots, weight, out, dst in levels:
        field = buf[w : w * (h + 1)].astype(F32) + dot(spots[...], g.rs2[...])
        rows = [
            field[0:w] + g.from_n[at : at + w].astype(F32),
            field[w : w * (h - 1)],
            field[w * (h - 1) :] + g.from_s[at : at + w].astype(F32),
        ]
        whole = jnp.concatenate([part for part in rows if part.shape[0]], 0).astype(BF)
        out[...] = dot_t(whole, weight).astype(BF)
        store(out, dst)

    received(swap)
    cross = g.z2r[...].astype(F32)
    first = core == 0
    both = jnp.concatenate([jnp.where(first, same, cross), jnp.where(first, cross, same)], 0)
    o_conv[...] = jnp.where(first, both[:, 0:36], pltpu.roll(both, LANE - 36, 1)[:, 0:36])
    g.turn[...] = jnp.concatenate([both, jnp.zeros((96, LANE), F32)], 0).T
    o_lat[...] = jnp.where(first, g.turn[72:84, 0:32], g.turn[84:96, 0:32])

    for copy in sent:
        copy.wait_send()
    wait(stores)


VM = pltpu.VMEM
DMA = pltpu.SemaphoreType.DMA
SCRATCH = dict(
    finx=VM((768, C), BF),
    midx=VM((256, C), BF),
    coax=VM((128, C), BF),
    coab=VM((128, C), BF),
    v_wl=VM((768, C), BF),
    v_wo=VM((2304, C), BF),
    v_cot=VM((512, C), BF),
    v_u1=VM((224, 128), BF),
    v_u2=VM((672, 256), BF),
    v_d1=VM((224, 768), BF),
    v_d2=VM((96, 256), BF),
    v_pf=VM((32, 512), BF),
    v_pm=VM((32, 128), BF),
    v_pc=VM((32, 128), BF),
    v_s1=VM((96, 128), BF),
    topb=VM((128, C), BF),
    midb=VM((256, C), BF),
    fex=VM((672, C), F32),
    shift=VM((10, 80, C), F32),
    fsh=VM((640, 768), BF),
    dsh=VM((768, 768), BF),
    shift0=VM((12, 80, C), F32),
    rims=VM((96, C), BF),
    dtx=VM((96, C), BF),
    rows_n=VM((112, C), BF),
    rows_s=VM((112, C), BF),
    from_n=VM((112, C), BF),
    from_s=VM((112, C), BF),
    cols_w=VM((48, C), BF),
    cols_e=VM((48, C), BF),
    v_rim=VM((96, 512), BF),
    v_tf=VM((512, 384), BF),
    v_tm=VM((128, 384), BF),
    v_tc=VM((32, 384), BF),
    pre=VM((512, C), F32),
    maskb=VM((512, C), BF),
    dpx=VM((512, C), BF),
    dfx=VM((768, C), BF),
    dmx=VM((256, C), BF),
    fgb=VM((512, C), BF),
    mgb=VM((128, C), BF),
    cgb=VM((32, C), BF),
    pk1=VM((32, C), BF),
    rs1=VM((128, C), BF),
    rs2=VM((384, C), BF),
    grad=VM((8, 2, 16, 2304), BF),
    got=VM((8, 16, 2304), BF),
    lgrad=VM((8, 2, 16, 768), BF),
    lgot=VM((8, 16, 768), BF),
    cp1=VM((4, 4, 16, CP), BF),
    cp1r=VM((3, 4, 16, CP), BF),
    cp2=VM((4, 16, CP), BF),
    cp2r=VM((3, 16, CP), BF),
    cq1=VM((4, 4, 16, CQ), BF),
    cq1r=VM((3, 4, 16, CQ), BF),
    cq2=VM((4, 16, CQ), BF),
    cq2r=VM((3, 16, CQ), BF),
    lp1=VM((4, 4, 16, LP), BF),
    lp1r=VM((3, 4, 16, LP), BF),
    lp2=VM((4, 16, LP), BF),
    lp2r=VM((3, 16, LP), BF),
    lq1=VM((4, 4, 16, LQ), BF),
    lq1r=VM((3, 4, 16, LQ), BF),
    lq2=VM((4, 16, LQ), BF),
    lq2r=VM((3, 16, LQ), BF),
    sums=VM((16, 1536), F32),
    z1=VM((16, 16, LANE), BF),
    z1r=VM((15, 16, LANE), BF),
    z2=VM((16, LANE), BF),
    z2r=VM((16, LANE), BF),
    far=pltpu.SemaphoreType.REGULAR((3,)),
    v_a1=VM((768, 256), BF),
    v_a2=VM((768, 128), BF),
    turn=VM((128, 128), F32),
    lsem=DMA((24,)),
    osem=DMA((4,)),
    ssem=DMA((96,)),
    rsem=DMA((96,)),
)


def hand_on(*refs):
    n = len(refs) // 3
    ins, outs, held, sems = refs[:n], refs[n : 2 * n], refs[2 * n : 3 * n], refs[3 * n]
    arrive = [pltpu.make_async_copy(ins[i], held[i], sems.at[0, i]) for i in range(n)]
    leave = [pltpu.make_async_copy(held[i], outs[i], sems.at[1, i]) for i in range(n)]
    for copy in arrive:
        copy.start()
    for i in reversed(range(n)):
        arrive[i].wait()
        leave[i].start()
    for copy in leave:
        copy.wait()


def local(consts, fine_in, mid_in, coarse_in, lateral_weight, out_weight, cotangent):
    def flat(v):
        return v.reshape(-1, v.shape[-1])

    args = [flat(fine_in), flat(mid_in), flat(coarse_in), lateral_weight, out_weight, flat(cotangent)]
    args += [jnp.asarray(v) for v in consts.values()]
    hbm = pl.BlockSpec(memory_space=pl.ANY)
    vmem = pl.BlockSpec(memory_space=pltpu.VMEM)
    outs = pl.pallas_call(
        functools.partial(kernel, tuple(consts)),
        out_shape=[
            jax.ShapeDtypeStruct((512, C), BF),
            jax.ShapeDtypeStruct((512, C), BF),
            jax.ShapeDtypeStruct((128, C), BF),
            jax.ShapeDtypeStruct((32, C), BF),
            jax.ShapeDtypeStruct((12, 32), F32),
            jax.ShapeDtypeStruct((32, 36), F32),
        ],
        in_specs=[hbm] * len(args),
        out_specs=[hbm] * 4 + [vmem] * 2,
        scratch_shapes=list(SCRATCH.values()),
        compiler_params=pltpu.CompilerParams(
            collective_id=0, has_side_effects=True, vmem_limit_bytes=63 * 2**20
        ),
        cost_estimate=pl.CostEstimate(flops=2_400_000_000, bytes_accessed=4_000_000, transcendentals=262144),
    )(*args)
    outs = pl.pallas_call(
        hand_on,
        out_shape=[jax.ShapeDtypeStruct(v.shape, v.dtype) for v in outs],
        in_specs=[hbm] * len(outs),
        out_specs=[hbm] * len(outs),
        scratch_shapes=[VM(v.shape, v.dtype) for v in outs] + [DMA((2, len(outs)))],
        compiler_params=pltpu.CompilerParams(vmem_limit_bytes=63 * 2**20),
    )(*outs)
    return (
        outs[0].reshape(fine_in.shape),
        outs[1].reshape(fine_in.shape),
        outs[2].reshape(mid_in.shape),
        outs[3].reshape(coarse_in.shape),
        outs[4],
        outs[5].T,
    )


def solution(mesh):
    field = P("rows", "cols", None)
    return jax.shard_map(
        functools.partial(local, constants()),
        mesh=mesh,
        in_specs=(field, field, field, P(), P(), field),
        out_specs=(field, field, field, field, P("cols", "rows"), P("cols", "rows")),
        check_vma=False,
    )
```
